32 devices in a mesh: groups: 2 (over y), adapter: 4 (over z), lane: 4 (over x, core).
Axes of the slice: x: 2, y: 2, z: 4, core: 2. Of those that a mesh axis runs over, the one named last changes fastest.
Arguments:
- residual_input: bfloat16 [128, 8192], P(('groups', 'adapter')), parts along dimension 0, may hold values from -6 to 6
- attention_norm_gain: float32 [8192], replicated, may hold values from 0.25 to 1.75
- query_weight: bfloat16 [8192, 8192], P('adapter', 'lane'), may hold values from -0.0625 to 0.0625
- key_weight: bfloat16 [8192, 1024], P('adapter', 'lane'), may hold values from -0.0625 to 0.0625
- value_weight: bfloat16 [8192, 1024], P('adapter', 'lane'), may hold values from -0.0625 to 0.0625
- query_down_weight: bfloat16 [8, 8192, 64], P('adapter', 'lane'), may hold values from -0.0625 to 0.0625
- query_up_weight: bfloat16 [8, 64, 8192], P('adapter', None, 'lane'), may hold values from -0.75 to 0.75
- value_down_weight: bfloat16 [8, 8192, 64], P('adapter', 'lane'), may hold values from -0.0625 to 0.0625
- value_up_weight: bfloat16 [8, 64, 1024], P('adapter', None, 'lane'), may hold values from -0.75 to 0.75
- cached_key_rows: bfloat16 [128, 8, 256, 128], P(('groups', 'adapter'), 'lane'), parts along dimension 0, may hold values from -200 to 200
- cached_value_rows: bfloat16 [128, 8, 256, 128], P(('groups', 'adapter'), 'lane'), parts along dimension 0, may hold values from -6 to 6
- row_adapter_index: int32 [128], P('groups'), parts along dimension 0, may hold values from 0 to 7, as said below
- cached_length: int32 [128], P(('groups', 'adapter')), parts along dimension 0, may hold values from 1 to 256, as said below
Outputs:
- attended: bfloat16 [128, 8192], P(('groups', 'adapter'), 'lane'), parts along dimension 0
- fresh_kv: bfloat16 [128, 2, 1024], P(('groups', 'adapter'), None, 'lane'), parts along dimension 0
The draws below stay inside these ranges and needn't reach their ends.
There are 2 independent parts, one for each index of `groups`. The reference program is written for one: setup_inputs(seed, part) draws one part's arguments, and reference() takes and returns one part's arrays. A program takes and returns all parts, laid end to end along the dimension named above; an argument that names none is the same for every part. Nothing has to cross between parts.
Inputs may be any that keep to these rules, and one draw needn't show every extreme that they name: `row_adapter_index`: rows come in aligned blocks of 16, one block per index of adapter. Adapter a belongs to owner a // 2. No block has more than 8 rows whose adapters belong to one owner, and in every block some owner has exactly 8. `cached_length`: some row has exactly 256 cached positions.
All inputs are finite; a program needn't handle non-finite values.
Results may differ from the reference program's by a relative error of at most 0.029.
Values may be sent and summed in bfloat16 or wider, within the bound.
No kernel may reach another device: no remote copies, remote signals or barrier semaphores. Data moves between devices by JAX's collectives and lax.ppermute only.
A program may use at most 64 MiB of HBM per device.

```python
import jax
import jax.numpy as jnp
from jax import lax

MODEL_WIDTH = 8192
QUERY_HEADS = 64
KEY_VALUE_HEADS = 8
HEAD_SIZE = 128
ADAPTER_RANK = 64
ADAPT_DEV = 2
ROWS_DEV = 16
CONTEXT = 256
ADAPTER_COUNT = 8
ROWS = 64
CAP = 8
HOT = 1


def draw_row_adapter_index(key, part):
    key = jax.random.fold_in(key, 11)
    owners_count = ROWS // ROWS_DEV
    order_key, block_key, local_key = jax.random.split(key, 3)
    order = jax.random.permutation(order_key, owners_count)
    cold_count = owners_count - HOT

    def one_block(block_seed):
        key_one, key_two, key_three, key_four = jax.random.split(block_seed, 4)
        hot_taken = jax.random.randint(key_one, (), 1, HOT + 1)
        hot_pick = order[jax.random.permutation(key_two, HOT)]
        cold_pick = order[HOT + jax.random.permutation(key_three, cold_count)]
        position = jnp.arange(ROWS_DEV)
        filled = hot_taken * CAP
        hot_owner = hot_pick[jnp.minimum(position // CAP, HOT - 1)]
        cold_owner = cold_pick[jnp.maximum(position - filled, 0) % cold_count]
        owner = jnp.where(position < filled, hot_owner, cold_owner)
        return owner[jax.random.permutation(key_four, ROWS_DEV)]
    owners = jax.vmap(one_block)(jax.random.split(block_key, owners_count)).reshape(ROWS)
    local_pick = jax.random.randint(local_key, (ROWS,), 0, ADAPT_DEV)
    return (owners * ADAPT_DEV + local_pick).astype(jnp.int32)


def draw_cached_length(key, part):
    key = jax.random.fold_in(key, 23)
    key_one, key_two = jax.random.split(key)
    lengths = jax.random.randint(key_one, (ROWS,), 1, CONTEXT + 1)
    longest = jax.random.randint(key_two, (), 0, ROWS)
    return jnp.where(jnp.arange(ROWS) == longest, CONTEXT, lengths).astype(jnp.int32)


def draw_cached_key_rows(key, part):
    key = jax.random.fold_in(key, 37)
    key_one = jax.random.fold_in(key, 0)
    values = jax.random.normal(key_one, (ROWS, KEY_VALUE_HEADS, CONTEXT, HEAD_SIZE), jnp.float32)
    values = jnp.clip(values, -6.0, 6.0)
    return values.astype(jnp.bfloat16)


def steps_of(key, extent, shards, low, high):
    def one(axis_at, parts):
        draws = jax.random.uniform(jax.random.fold_in(jax.random.fold_in(key, 6), axis_at), (parts,), jnp.float32, low / len(shards), high / len(shards))
        return jnp.repeat(jnp.exp(draws), extent[axis_at] // parts).reshape((-1,) + (1,) * (len(extent) - axis_at - 1))

    loudness = one(*shards[0])
    for cut in shards[1:]:
        loudness = loudness * one(*cut)
    return loudness


def bell_draw(rng, shape, scale, most, cuts=(), held_as=jnp.bfloat16):
    entries = jax.random.normal(rng, shape, jnp.float32) * scale
    if len(cuts) > 0:
        entries = steps_of(rng, shape, cuts, -0.22, 0.18) * entries
    return jnp.clip(entries, min=-most, max=most).astype(held_as)


def setup_inputs(seed: int = 0, part: int = 0) -> dict:
    key_of = jax.random.split(jax.random.key(seed), 14)
    own_keys = jax.random.split(jax.random.fold_in(key_of[13], part), 14)
    residual_input = bell_draw(own_keys[0], (ROWS, MODEL_WIDTH), 1.0, 6.0, ((0, 4),))
    attention_norm_gain = jnp.clip(1.0 + 0.15 * jax.random.normal(key_of[1], (MODEL_WIDTH,), jnp.float32), 0.25, 1.75)
    query_weight = bell_draw(key_of[2], (MODEL_WIDTH, QUERY_HEADS * HEAD_SIZE), MODEL_WIDTH ** -0.5, 0.0625, ((0, 4), (1, 4)))
    key_weight = bell_draw(key_of[3], (MODEL_WIDTH, KEY_VALUE_HEADS * HEAD_SIZE), MODEL_WIDTH ** -0.5, 0.0625, ((0, 4), (1, 4)))
    value_weight = bell_draw(key_of[4], (MODEL_WIDTH, KEY_VALUE_HEADS * HEAD_SIZE), MODEL_WIDTH ** -0.5, 0.0625, ((0, 4), (1, 4)))
    query_down_weight = bell_draw(key_of[5], (ADAPTER_COUNT, MODEL_WIDTH, ADAPTER_RANK), MODEL_WIDTH ** -0.5, 0.0625, ((0, 4), (1, 4)))
    query_up_weight = bell_draw(key_of[6], (ADAPTER_COUNT, ADAPTER_RANK, QUERY_HEADS * HEAD_SIZE), ADAPTER_RANK ** -0.5, 0.75, ((0, 4), (2, 4)))
    value_down_weight = bell_draw(key_of[7], (ADAPTER_COUNT, MODEL_WIDTH, ADAPTER_RANK), MODEL_WIDTH ** -0.5, 0.0625, ((0, 4), (1, 4)))
    value_up_weight = bell_draw(key_of[8], (ADAPTER_COUNT, ADAPTER_RANK, KEY_VALUE_HEADS * HEAD_SIZE), ADAPTER_RANK ** -0.5, 0.75, ((0, 4), (2, 4)))
    cached_key_rows = draw_cached_key_rows(jax.random.fold_in(jax.random.fold_in(key_of[13], part), 71), part)
    cached_value_rows = bell_draw(own_keys[10], (ROWS, KEY_VALUE_HEADS, CONTEXT, HEAD_SIZE), 1.0, 6.0, ((0, 4), (1, 4)))
    row_adapter_index = draw_row_adapter_index(jax.random.fold_in(jax.random.fold_in(key_of[13], part), 71), part)
    cached_length = draw_cached_length(jax.random.fold_in(jax.random.fold_in(key_of[13], part), 71), part)
    return {"residual_input": residual_input, "attention_norm_gain": attention_norm_gain, "query_weight": query_weight, "key_weight": key_weight, "value_weight": value_weight, "query_down_weight": query_down_weight, "query_up_weight": query_up_weight, "value_down_weight": value_down_weight, "value_up_weight": value_up_weight, "cached_key_rows": cached_key_rows, "cached_value_rows": cached_value_rows, "row_adapter_index": row_adapter_index, "cached_length": cached_length}


EPS = 1e-05
ADAPTER_SCALE = 0.5

def adapter_updates(normalized_input, row_adapter_index, query_down_weight, query_up_weight, value_down_weight, value_up_weight):

    def one_row(pair):
        row_vec, selected_adapter = pair
        selected_adapter = selected_adapter.astype(jnp.int32)
        query_down_matrix = lax.dynamic_index_in_dim(query_down_weight, selected_adapter, 0, keepdims=False)
        query_up_matrix = lax.dynamic_index_in_dim(query_up_weight, selected_adapter, 0, keepdims=False)
        value_down_matrix = lax.dynamic_index_in_dim(value_down_weight, selected_adapter, 0, keepdims=False)
        value_up_matrix = lax.dynamic_index_in_dim(value_up_weight, selected_adapter, 0, keepdims=False)
        query_down_rows = jnp.dot(row_vec[None, :], query_down_matrix, preferred_element_type=jnp.float32).astype(jnp.bfloat16)
        value_down_rows = jnp.dot(row_vec[None, :], value_down_matrix, preferred_element_type=jnp.float32).astype(jnp.bfloat16)
        query_update = (ADAPTER_SCALE * jnp.dot(query_down_rows, query_up_matrix, preferred_element_type=jnp.float32)).astype(jnp.bfloat16)
        value_update = (ADAPTER_SCALE * jnp.dot(value_down_rows, value_up_matrix, preferred_element_type=jnp.float32)).astype(jnp.bfloat16)
        return (query_update[0], value_update[0])
    return lax.map(one_row, (normalized_input, row_adapter_index))

def reference(residual_input, attention_norm_gain, query_weight, key_weight, value_weight, query_down_weight, query_up_weight, value_down_weight, value_up_weight, cached_key_rows, cached_value_rows, row_adapter_index, cached_length):
    widened = residual_input.astype(jnp.float32)
    normalized_input = (widened * lax.rsqrt(lax.optimization_barrier(jnp.mean(widened * widened, axis=-1, keepdims=True)) + EPS) * attention_norm_gain).astype(jnp.bfloat16)
    query_update, value_update = adapter_updates(normalized_input, row_adapter_index, query_down_weight, query_up_weight, value_down_weight, value_up_weight)
    queries = (jnp.dot(normalized_input, query_weight, preferred_element_type=jnp.float32) + query_update.astype(jnp.float32)).astype(jnp.bfloat16)
    key_new = jnp.dot(normalized_input, key_weight, preferred_element_type=jnp.float32).astype(jnp.bfloat16)
    value_new = (jnp.dot(normalized_input, value_weight, preferred_element_type=jnp.float32) + value_update.astype(jnp.float32)).astype(jnp.bfloat16)
    fresh_kv = jnp.stack([key_new, value_new], axis=1)
    group_size = QUERY_HEADS // KEY_VALUE_HEADS
    scale = HEAD_SIZE ** (-0.5)
    grouped = queries.reshape(ROWS, KEY_VALUE_HEADS, group_size, HEAD_SIZE).astype(jnp.float32)
    key_heads = key_new.reshape(ROWS, KEY_VALUE_HEADS, HEAD_SIZE).astype(jnp.float32)
    value_heads = value_new.reshape(ROWS, KEY_VALUE_HEADS, 1, HEAD_SIZE).astype(jnp.float32)
    scores = jnp.einsum('rkgd,rksd->rkgs', grouped, cached_key_rows.astype(jnp.float32)) * scale
    own_score = jnp.einsum('rkgd,rkd->rkg', grouped, key_heads) * scale
    visible = jnp.arange(CONTEXT)[None, None, None, :] < cached_length[:, None, None, None]
    peak = jnp.maximum(lax.optimization_barrier(jnp.max(jnp.where(visible, scores, -jnp.inf), axis=-1)), own_score)
    lifted = jnp.where(visible, jnp.exp(scores - peak[..., None]), 0.0)
    own_lift = jnp.exp(own_score - peak)
    row_total = lax.optimization_barrier(jnp.sum(lifted, axis=-1)) + own_lift
    weights = (lifted / row_total[..., None]).astype(jnp.bfloat16)
    own_weight = (own_lift / row_total).astype(jnp.bfloat16)
    mixed = jnp.einsum('rkgs,rksd->rkgd', weights.astype(jnp.float32), cached_value_rows.astype(jnp.float32))
    mixed = mixed + own_weight.astype(jnp.float32)[..., None] * value_heads
    attended = mixed.reshape(ROWS, QUERY_HEADS * HEAD_SIZE).astype(jnp.bfloat16)
    return (attended, fresh_kv)
```

```python
import jax
import jax.numpy as jnp
from jax import lax
from jax.sharding import PartitionSpec as P

EPS = 1e-05
ADAPTER_SCALE = 0.5


def partner(array, axis, step):
    count = lax.axis_size(axis)
    return lax.ppermute(array, axis, [(i, i ^ step) for i in range(count)])


def on_device(
    residual_input,
    attention_norm_gain,
    query_weight,
    key_weight,
    value_weight,
    query_down_weight,
    query_up_weight,
    value_down_weight,
    value_up_weight,
    cached_key_rows,
    cached_value_rows,
    row_adapter_index,
    cached_length,
):
    owners_count = lax.axis_size("adapter")
    lane_count = lax.axis_size("lane")
    my_index = lax.axis_index("adapter")
    lane_index = lax.axis_index("lane")
    block_rows, width = residual_input.shape
    nearby_count, _, rank = query_down_weight.shape
    capacity = max(2, 2 * block_rows // owners_count)
    lane_width = width // lane_count
    base_width = width // owners_count
    query_cols = query_weight.shape[1]
    kv_cols = key_weight.shape[1]
    steps = range(owners_count)

    order = jnp.bitwise_xor(my_index, jnp.arange(owners_count))
    blocks = row_adapter_index.reshape(owners_count, block_rows)

    def slot_map(ids, owner):
        hit = (ids // nearby_count == owner).astype(jnp.int32)
        place = jnp.cumsum(hit) - hit
        return (jnp.arange(capacity)[:, None] == place[None, :]) & (hit[None, :] > 0)

    mine = lax.dynamic_index_in_dim(blocks, my_index, 0, keepdims=False)
    lane_part = lax.dynamic_slice_in_dim(residual_input, lane_index * lane_width, lane_width, 1)
    base_rows, adapter_rows = [], []
    for step in steps:
        other = my_index ^ step
        base = lax.dynamic_slice_in_dim(residual_input, other * base_width, base_width, 1)
        placed = jnp.dot(
            slot_map(mine, other).astype(jnp.bfloat16), lane_part, preferred_element_type=jnp.float32
        ).astype(jnp.bfloat16)
        if step == 0:
            base_rows.append(base)
            adapter_rows.append(placed)
        elif base_width == lane_width:
            both = partner(jnp.concatenate([base, placed], axis=0), "adapter", step)
            base_rows.append(both[:block_rows])
            adapter_rows.append(both[block_rows:])
        else:
            base_rows.append(partner(base, "adapter", step))
            adapter_rows.append(partner(placed, "adapter", step))

    base_gain = lax.dynamic_slice_in_dim(attention_norm_gain, my_index * base_width, base_width, 0)
    lane_gain = lax.dynamic_slice_in_dim(attention_norm_gain, lane_index * lane_width, lane_width, 0)

    gained = (jnp.concatenate(adapter_rows, axis=0).astype(jnp.float32) * lane_gain).astype(
        jnp.bfloat16
    )
    down_parts = []
    for weight in (query_down_weight, value_down_weight):
        down_parts.append(
            jnp.einsum("xi,yig->xyg", gained, weight, preferred_element_type=jnp.float32)
        )
    down = jnp.concatenate(down_parts, axis=2)
    seen = lax.dynamic_index_in_dim
    row_maps, row_hot = [], []
    for step in steps:
        ids = seen(blocks, my_index ^ step, 0, keepdims=False)
        row_maps.append(slot_map(ids, my_index))
        row_hot.append(ids[:, None] == my_index * nearby_count + jnp.arange(nearby_count)[None, :])
    maps = jnp.stack(row_maps).astype(jnp.float32)
    hot = jnp.concatenate(row_hot, axis=0)
    slots = down.reshape(owners_count, capacity, nearby_count, 2 * rank)
    slot_hot = jnp.einsum(
        "bsr,brg->bsg", maps, hot.reshape(owners_count, block_rows, nearby_count).astype(jnp.float32)
    )
    chosen = jnp.sum(slots * slot_hot[..., None], axis=2).reshape(owners_count * capacity, 2 * rank)
    total = chosen
    for step in range(1, lane_count):
        total = total + partner(chosen, "lane", step)

    rows = (jnp.concatenate(base_rows, axis=0).astype(jnp.float32) * base_gain).astype(jnp.bfloat16)
    base_q = jnp.dot(rows, query_weight, preferred_element_type=jnp.float32)
    base_k = jnp.dot(rows, key_weight, preferred_element_type=jnp.float32)
    base_v = jnp.dot(rows, value_weight, preferred_element_type=jnp.float32)

    low = total.astype(jnp.bfloat16).reshape(owners_count, capacity, 2 * rank)
    low = jnp.einsum(
        "bsr,bsg->brg", maps.astype(jnp.bfloat16), low, preferred_element_type=jnp.float32
    ).astype(jnp.bfloat16).reshape(owners_count * block_rows, 2 * rank)
    hot_low = hot.astype(jnp.bfloat16)
    low_q = (low[:, None, :rank] * hot_low[:, :, None]).reshape(-1, nearby_count * rank)
    low_v = (low[:, None, rank:] * hot_low[:, :, None]).reshape(-1, nearby_count * rank)
    base_q = base_q + ADAPTER_SCALE * jnp.dot(
        low_q, query_up_weight.reshape(-1, query_cols), preferred_element_type=jnp.float32
    )
    base_v = base_v + ADAPTER_SCALE * jnp.dot(
        low_v, value_up_weight.reshape(-1, kv_cols), preferred_element_type=jnp.float32
    )
    summand = jnp.concatenate([base_q, base_k, base_v], axis=1)
    summed = summand[:block_rows]
    for step in range(1, owners_count):
        part = summand[step * block_rows : (step + 1) * block_rows].astype(jnp.bfloat16)
        summed = summed + partner(part, "adapter", step).astype(jnp.float32)
    widened = residual_input.astype(jnp.float32)
    scaling = lax.rsqrt(jnp.mean(widened * widened, axis=-1, keepdims=True) + EPS)
    summed = summed * scaling

    queries = summed[:, :query_cols].astype(jnp.bfloat16)
    key_new = summed[:, query_cols : query_cols + kv_cols].astype(jnp.bfloat16)
    value_new = summed[:, query_cols + kv_cols :].astype(jnp.bfloat16)
    fresh_kv = jnp.stack([key_new, value_new], axis=1)
    kv_local = cached_key_rows.shape[1]
    head_dim = cached_key_rows.shape[3]
    context = cached_key_rows.shape[2]
    group_size = query_cols // head_dim // kv_local
    scale = head_dim ** (-0.5)
    grouped = queries.reshape(block_rows, kv_local, group_size, head_dim)
    key_heads = key_new.reshape(block_rows, kv_local, head_dim)
    value_heads = value_new.reshape(block_rows, kv_local, 1, head_dim).astype(jnp.float32)
    scores = (
        jnp.einsum("rkgd,rksd->rkgs", grouped, cached_key_rows, preferred_element_type=jnp.float32)
        * scale
    )
    own_score = (
        jnp.einsum("rkgd,rkd->rkg", grouped, key_heads, preferred_element_type=jnp.float32) * scale
    )
    visible = jnp.arange(context)[None, None, None, :] < cached_length[:, None, None, None]
    peak = jnp.maximum(jnp.max(jnp.where(visible, scores, -jnp.inf), axis=-1), own_score)
    lifted = jnp.where(visible, jnp.exp(scores - peak[..., None]), 0.0)
    own_lift = jnp.exp(own_score - peak)
    row_total = jnp.sum(lifted, axis=-1) + own_lift
    weights = (lifted / row_total[..., None]).astype(jnp.bfloat16)
    own_weight = (own_lift / row_total).astype(jnp.bfloat16)
    mixed = jnp.einsum(
        "rkgs,rksd->rkgd", weights, cached_value_rows, preferred_element_type=jnp.float32
    )
    mixed = mixed + own_weight.astype(jnp.float32)[..., None] * value_heads
    attended = mixed.reshape(block_rows, query_cols).astype(jnp.bfloat16)
    return (attended, fresh_kv)


def solution(mesh):
    in_specs = (
        P(("groups", "adapter"), None),
        P(),
        P("adapter", "lane"),
        P("adapter", "lane"),
        P("adapter", "lane"),
        P("adapter", "lane", None),
        P("adapter", None, "lane"),
        P("adapter", "lane", None),
        P("adapter", None, "lane"),
        P(("groups", "adapter"), "lane", None, None),
        P(("groups", "adapter"), "lane", None, None),
        P("groups"),
        P(("groups", "adapter")),
    )
    out_specs = (P(("groups", "adapter"), "lane"), P(("groups", "adapter"), None, "lane"))
    return jax.shard_map(
        on_device, mesh=mesh, in_specs=in_specs, out_specs=out_specs, check_vma=False
    )
```

```python
import jax
import jax.numpy as jnp
from jax import lax
from jax.experimental import pallas as pl
from jax.experimental.pallas import tpu as pltpu
from jax.sharding import PartitionSpec as P

EPS = 1e-05
ADAPTER_SCALE = 0.5
MIB = 2**20
F32 = jnp.float32
BF16 = jnp.bfloat16
VMEM = pl.BlockSpec(memory_space=pltpu.VMEM)
SMEM = pl.BlockSpec(memory_space=pltpu.SMEM)
HBM = pl.BlockSpec(memory_space=pltpu.HBM)


def partner(array, axis, step):
    count = lax.axis_size(axis)
    return lax.ppermute(array, axis, [(i, i ^ step) for i in range(count)])


def call(body, name, outs, in_specs, out_specs, args, scratch=(), limit=16, flops=0, moved=0):
    return pl.pallas_call(
        body,
        name=name,
        out_shape=outs,
        in_specs=in_specs,
        out_specs=out_specs,
        scratch_shapes=scratch,
        compiler_params=pltpu.CompilerParams(vmem_limit_bytes=limit * MIB),
        cost_estimate=pl.CostEstimate(flops=flops, bytes_accessed=moved, transcendentals=0),
    )(*args)


def iota(shape, axis):
    return lax.broadcasted_iota(jnp.int32, shape, axis)


def slot_map(ids, owner, block, capacity, block_rows, nearby):
    slots, rows = owner.shape[0], ids.shape[1]
    first = owner * nearby
    spot = iota((slots, rows), 1)
    hit = (ids >= first) & (ids < first + nearby)
    hit = hit & (spot >= block * block_rows) & (spot < (block + 1) * block_rows)
    before = (iota((rows, rows), 0) < iota((rows, rows), 1)).astype(BF16)
    place = jnp.dot(
        jnp.where(hit, 1.0, 0.0).astype(BF16), before, preferred_element_type=F32
    )
    which = lax.rem(iota((slots, rows), 0), capacity).astype(F32)
    return jnp.where(hit & (place == which), 1.0, 0.0)


def on_device(
    residual_input,
    attention_norm_gain,
    query_weight,
    key_weight,
    value_weight,
    query_down_weight,
    query_up_weight,
    value_down_weight,
    value_up_weight,
    cached_key_rows,
    cached_value_rows,
    row_adapter_index,
    cached_length,
):
    owners_count = lax.axis_size("adapter")
    lane_count = lax.axis_size("lane")
    block_rows, width = residual_input.shape
    nearby, _, rank = query_down_weight.shape
    capacity = max(2, 2 * block_rows // owners_count)
    lane_width = width // lane_count
    base_width = width // owners_count
    query_cols = query_weight.shape[1]
    kv_cols = key_weight.shape[1]
    all_cols = query_cols + 2 * kv_cols
    slots = owners_count * capacity
    rows = owners_count * block_rows
    low_cols = nearby * rank
    joined = base_width == lane_width
    kv_local, context, head_dim = cached_key_rows.shape[1:]
    group_size = query_cols // head_dim // kv_local
    heads = kv_local * group_size

    ids = row_adapter_index.reshape(1, rows)
    gain = attention_norm_gain.reshape(1, width)
    query_down = jnp.swapaxes(query_down_weight, 1, 2).reshape(low_cols, lane_width)
    value_down = jnp.swapaxes(value_down_weight, 1, 2).reshape(low_cols, lane_width)
    query_up = query_up_weight.reshape(low_cols, query_cols)
    value_up = value_up_weight.reshape(low_cols, kv_cols)

    def prepare(ids_ref, x_ref, *out_refs):
        me = lax.axis_index("adapter")
        lane = lax.axis_index("lane")
        owner = jnp.bitwise_xor(me, iota((slots, 1), 0) // capacity)
        chosen = slot_map(
            ids_ref[...], owner, jnp.full((slots, 1), me), capacity, block_rows, nearby
        )
        fold = lax.rem(iota((rows, block_rows), 0), block_rows) == iota((rows, block_rows), 1)
        chosen = jnp.dot(
            chosen.astype(BF16), jnp.where(fold, 1.0, 0.0).astype(BF16), preferred_element_type=F32
        )
        part = x_ref[:, pl.ds(pl.multiple_of(lane * lane_width, lane_width), lane_width)]
        placed = jnp.dot(chosen.astype(BF16), part, preferred_element_type=F32)
        for step in range(owners_count):
            other = jnp.bitwise_xor(me, step)
            base = x_ref[:, pl.ds(pl.multiple_of(other * base_width, base_width), base_width)]
            mine = placed[step * capacity : (step + 1) * capacity].astype(BF16)
            if joined:
                out_refs[step][...] = jnp.concatenate([base, mine], axis=0)
            else:
                out_refs[2 * step][...] = base
                out_refs[2 * step + 1][...] = mine

    if joined:
        shapes = [jax.ShapeDtypeStruct((block_rows + capacity, base_width), BF16)] * owners_count
    else:
        shapes = [
            jax.ShapeDtypeStruct((block_rows, base_width), BF16),
            jax.ShapeDtypeStruct((capacity, lane_width), BF16),
        ] * owners_count
    sent = call(
        prepare, "prepare", shapes, [VMEM] * 2, [VMEM] * len(shapes), (ids, residual_input),
        moved=2**19,
    )
    per = len(sent) // owners_count
    arrived = list(sent[:per])
    for step in range(1, owners_count):
        for piece in sent[per * step : per * (step + 1)]:
            arrived.append(partner(piece, "adapter", step))

    held = (
        query_weight, key_weight, value_weight, query_down, value_down, query_up, value_up,
        cached_key_rows, cached_value_rows,
    )

    def fetch(x_ref, *refs):
        sources, targets, rms_ref, sems = refs[: len(held)], refs[len(held) : -2], refs[-2], refs[-1]
        copies = [
            pltpu.make_async_copy(source, target, sems.at[i])
            for i, (source, target) in enumerate(zip(sources, targets))
        ]
        for copy in copies:
            copy.start()
        x = x_ref[...].astype(F32)
        mean = jnp.sum(x * x, axis=1, keepdims=True) * (1.0 / width)
        rms_ref[...] = jnp.broadcast_to(lax.rsqrt(mean + EPS), rms_ref.shape)
        for copy in copies:
            copy.wait()

    fetched = call(
        fetch,
        "fetch",
        [pltpu.VMEM(a.shape, a.dtype) for a in held]
        + [jax.ShapeDtypeStruct((block_rows, 128), F32)],
        [VMEM] + [HBM] * len(held),
        [VMEM] * (len(held) + 1),
        (residual_input, *(pltpu.with_memory_space_constraint(a, pltpu.HBM) for a in held)),
        scratch=[pltpu.SemaphoreType.DMA((len(held),))],
        moved=16 * MIB,
    )
    (w_query, w_key, w_value, w_query_down, w_value_down, w_query_up, w_value_up,
     keys, values, row_scale) = fetched

    def base_of(refs, step):
        return refs[step][:block_rows, :] if joined else refs[2 * step][...]

    def slots_of(refs, step):
        return refs[step][block_rows:, :] if joined else refs[2 * step + 1][...]

    def lower(gain_ref, dq_ref, dv_ref, *refs):
        part_refs, out_ref = refs[:-1], refs[-1]
        lane = lax.axis_index("lane")
        scaled = gain_ref[:, pl.ds(pl.multiple_of(lane * lane_width, lane_width), lane_width)]
        taken = jnp.concatenate(
            [slots_of(part_refs, step).astype(F32) for step in range(owners_count)], axis=0
        )
        taken = (taken * scaled).astype(BF16)
        contract = (((1,), (1,)), ((), ()))
        out_ref[:, :low_cols] = lax.dot_general(
            taken, dq_ref[...], contract, preferred_element_type=F32
        )
        out_ref[:, low_cols:] = lax.dot_general(
            taken, dv_ref[...], contract, preferred_element_type=F32
        )

    low = call(
        lower, "lower", jax.ShapeDtypeStruct((slots, 2 * low_cols), F32),
        [VMEM] * (3 + len(arrived)), VMEM, (gain, w_query_down, w_value_down, *arrived), moved=MIB,
    )
    lows = [low] + [partner(low, "lane", step) for step in range(1, lane_count)]

    def project(gain_ref, wq_ref, wk_ref, wv_ref, *refs):
        part_refs, out_ref, x_ref = refs[:-2], refs[-2], refs[-1]
        me = lax.axis_index("adapter")
        scaled = gain_ref[:, pl.ds(pl.multiple_of(me * base_width, base_width), base_width)]
        for step in range(owners_count):
            start = pl.multiple_of(jnp.bitwise_xor(me, step) * block_rows, block_rows)
            x_ref[pl.ds(start, block_rows), :] = (
                base_of(part_refs, step).astype(F32) * scaled
            ).astype(BF16)
        tile = min(1024, query_cols)
        for at in range(0, query_cols, tile):
            out_ref[:, at : at + tile] = jnp.dot(
                x_ref[...], wq_ref[:, at : at + tile], preferred_element_type=F32
            )
        out_ref[:, query_cols : query_cols + kv_cols] = jnp.dot(
            x_ref[...], wk_ref[...], preferred_element_type=F32
        )
        out_ref[:, query_cols + kv_cols :] = jnp.dot(
            x_ref[...], wv_ref[...], preferred_element_type=F32
        )

    based = call(
        project, "project", jax.ShapeDtypeStruct((rows, all_cols), F32),
        [VMEM] * (4 + len(arrived)), VMEM, (gain, w_query, w_key, w_value, *arrived),
        scratch=[pltpu.VMEM((rows, base_width), BF16)],
        flops=2 * rows * base_width * all_cols, moved=10 * MIB,
    )

    def raise_up(ids_ref, based_ref, uq_ref, uv_ref, *refs):
        low_refs, out_refs, sum_ref = refs[:lane_count], refs[lane_count:-1], refs[-1]
        me = lax.axis_index("adapter")
        block = jnp.bitwise_xor(me, iota((slots, 1), 0) // capacity)
        seen = slot_map(
            ids_ref[...], jnp.full((slots, 1), me), block, capacity, block_rows, nearby
        )
        total = low_refs[0][...]
        for ref in low_refs[1:]:
            total = total + ref[...]
        column = lax.rem(iota((slots, 2 * low_cols), 1) // rank, nearby)
        picked = jnp.zeros_like(total)
        for near in range(nearby):
            uses = jnp.where(ids_ref[...] == me * nearby + near, seen, 0.0)
            uses = jnp.sum(uses, axis=1, keepdims=True) > 0.5
            picked = jnp.where(uses & (column == near), total, picked)
        lowered = lax.dot_general(
            seen.astype(BF16), picked.astype(BF16), (((0,), (0,)), ((), ())),
            preferred_element_type=F32,
        ).astype(BF16)
        for at in range(0, query_cols, 1024):
            stop = min(at + 1024, query_cols)
            sum_ref[:, at:stop] = based_ref[:, at:stop] + ADAPTER_SCALE * jnp.dot(
                lowered[:, :low_cols], uq_ref[:, at:stop], preferred_element_type=F32
            )
        middle = slice(query_cols, query_cols + kv_cols)
        last = slice(query_cols + kv_cols, all_cols)
        sum_ref[:, middle] = based_ref[:, middle]
        sum_ref[:, last] = based_ref[:, last] + ADAPTER_SCALE * jnp.dot(
            lowered[:, low_cols:], uv_ref[...], preferred_element_type=F32
        )
        for step in range(owners_count):
            start = pl.multiple_of(jnp.bitwise_xor(me, step) * block_rows, block_rows)
            out_refs[step][...] = sum_ref[pl.ds(start, block_rows), :].astype(out_refs[step].dtype)

    parts = call(
        raise_up, "raise_up",
        [
            jax.ShapeDtypeStruct((block_rows, all_cols), BF16 if step else F32)
            for step in range(owners_count)
        ],
        [VMEM] * (4 + lane_count), [VMEM] * owners_count,
        (ids, based, w_query_up, w_value_up, *lows),
        scratch=[pltpu.VMEM((rows, all_cols), F32)],
    )
    parts = [parts[0]] + [
        partner(parts[step], "adapter", step) for step in range(1, owners_count)
    ]

    def finish(length_ref, scale_ref, k_ref, v_ref, *refs):
        part_refs = refs[:owners_count]
        out_ref, fresh_ref, sum_ref, q_ref, s_ref, o_ref = refs[owners_count:]
        summed = part_refs[0][...]
        for ref in part_refs[1:]:
            summed = summed + ref[...].astype(F32)
        summed = (summed * scale_ref[:, :1]).astype(BF16)
        key_new = summed[:, query_cols : query_cols + kv_cols]
        value_new = summed[:, query_cols + kv_cols :]
        fresh_ref[:, :kv_cols] = key_new
        fresh_ref[:, kv_cols:] = value_new
        sum_ref[...] = summed.astype(F32)
        for head in range(heads):
            q_ref[:, head, :] = sum_ref[:, head * head_dim : (head + 1) * head_dim]
        scale = head_dim ** (-0.5)
        spot = iota((group_size, context), 1)
        own = []
        for row in range(block_rows):
            for group in range(kv_local):
                asked = q_ref[row, group * group_size : (group + 1) * group_size, :]
                scores = lax.dot_general(
                    asked.astype(BF16), k_ref[row, group], (((1,), (1,)), ((), ())),
                    preferred_element_type=F32,
                )
                s_ref[row * kv_local + group] = jnp.where(
                    spot < length_ref[row], scores * scale, -jnp.inf
                )
                at = query_cols + group * head_dim
                new = sum_ref[row : row + 1, at : at + head_dim]
                own.append(jnp.sum(asked * new, axis=1, keepdims=True))
        own_score = jnp.stack(own) * scale
        scores = s_ref[...]
        peak = jnp.maximum(jnp.max(scores, axis=2, keepdims=True), own_score)
        lifted = jnp.exp(scores - peak)
        own_lift = jnp.exp(own_score - peak)
        inverse = 1.0 / (jnp.sum(lifted, axis=2, keepdims=True) + own_lift)
        s_ref[...] = lifted * inverse
        own_weight = (own_lift * inverse).astype(BF16).astype(F32)
        for row in range(block_rows):
            for group in range(kv_local):
                index = row * kv_local + group
                mixed = jnp.dot(
                    s_ref[index].astype(BF16), v_ref[row, group], preferred_element_type=F32
                )
                at = query_cols + kv_cols + group * head_dim
                new = sum_ref[row : row + 1, at : at + head_dim]
                o_ref[row, group * group_size : (group + 1) * group_size, :] = (
                    mixed + own_weight[index] * new
                )
        for head in range(heads):
            out_ref[:, head * head_dim : (head + 1) * head_dim] = o_ref[:, head, :].astype(BF16)

    attended, fresh = call(
        finish, "finish",
        [
            jax.ShapeDtypeStruct((block_rows, query_cols), BF16),
            jax.ShapeDtypeStruct((block_rows, 2 * kv_cols), BF16),
        ],
        [SMEM] + [VMEM] * (3 + owners_count), [VMEM] * 2,
        (cached_length, row_scale, keys, values, *parts),
        scratch=[
            pltpu.VMEM((block_rows, all_cols), F32),
            pltpu.VMEM((block_rows, heads, head_dim), F32),
            pltpu.VMEM((block_rows * kv_local, group_size, context), F32),
            pltpu.VMEM((block_rows, heads, head_dim), F32),
        ],
    )
    return (attended, fresh.reshape(block_rows, 2, kv_cols))


def solution(mesh):
    in_specs = (
        P(("groups", "adapter"), None),
        P(),
        P("adapter", "lane"),
        P("adapter", "lane"),
        P("adapter", "lane"),
        P("adapter", "lane", None),
        P("adapter", None, "lane"),
        P("adapter", "lane", None),
        P("adapter", None, "lane"),
        P(("groups", "adapter"), "lane", None, None),
        P(("groups", "adapter"), "lane", None, None),
        P("groups"),
        P(("groups", "adapter")),
    )
    out_specs = (P(("groups", "adapter"), "lane"), P(("groups", "adapter"), None, "lane"))
    return jax.shard_map(
        on_device, mesh=mesh, in_specs=in_specs, out_specs=out_specs, check_vma=False
    )
```

```python
import jax
import jax.numpy as jnp
from jax import lax
from jax.experimental import pallas as pl
from jax.experimental.pallas import tpu as pltpu
from jax.sharding import PartitionSpec as P

EPS = 1e-05
ADAPTER_SCALE = 0.5
MIB = 2**20
F32 = jnp.float32
BF16 = jnp.bfloat16
VMEM = pl.BlockSpec(memory_space=pltpu.VMEM)
SMEM = pl.BlockSpec(memory_space=pltpu.SMEM)
HBM = pl.BlockSpec(memory_space=pltpu.HBM)


def partner(array, axis, step):
    count = lax.axis_size(axis)
    return lax.ppermute(array, axis, [(i, i ^ step) for i in range(count)])


def call(body, name, outs, in_specs, out_specs, args, scratch=(), limit=16, flops=0, moved=0):
    return pl.pallas_call(
        body,
        name=name,
        out_shape=outs,
        in_specs=in_specs,
        out_specs=out_specs,
        scratch_shapes=scratch,
        compiler_params=pltpu.CompilerParams(vmem_limit_bytes=limit * MIB),
        cost_estimate=pl.CostEstimate(flops=flops, bytes_accessed=moved, transcendentals=0),
    )(*args)


def in_hbm(array):
    return pltpu.with_memory_space_constraint(array, pltpu.HBM)


def iota(shape, axis):
    return lax.broadcasted_iota(jnp.int32, shape, axis)


def slot_map(ids, owner, block, capacity, block_rows, nearby):
    slots, rows = owner.shape[0], ids.shape[1]
    first = owner * nearby
    spot = iota((slots, rows), 1)
    hit = (ids >= first) & (ids < first + nearby)
    hit = hit & (spot >= block * block_rows) & (spot < (block + 1) * block_rows)
    before = (iota((rows, rows), 0) < iota((rows, rows), 1)).astype(BF16)
    place = jnp.dot(
        jnp.where(hit, 1.0, 0.0).astype(BF16), before, preferred_element_type=F32
    )
    which = lax.rem(iota((slots, rows), 0), capacity).astype(F32)
    return jnp.where(hit & (place == which), 1.0, 0.0)


def on_device(
    residual_input,
    attention_norm_gain,
    query_weight,
    key_weight,
    value_weight,
    query_down_weight,
    query_up_weight,
    value_down_weight,
    value_up_weight,
    cached_key_rows,
    cached_value_rows,
    row_adapter_index,
    cached_length,
):
    owners_count = lax.axis_size("adapter")
    lane_count = lax.axis_size("lane")
    block_rows, width = residual_input.shape
    nearby, _, rank = query_down_weight.shape
    capacity = max(2, 2 * block_rows // owners_count)
    lane_width = width // lane_count
    base_width = width // owners_count
    query_cols = query_weight.shape[1]
    kv_cols = key_weight.shape[1]
    all_cols = query_cols + 2 * kv_cols
    slots = owners_count * capacity
    rows = owners_count * block_rows
    low_cols = nearby * rank
    joined = base_width == lane_width
    kv_local, context, head_dim = cached_key_rows.shape[1:]
    group_size = query_cols // head_dim // kv_local
    heads = kv_local * group_size

    ids = row_adapter_index.reshape(1, rows)
    gain = attention_norm_gain.reshape(1, width)
    query_down = jnp.swapaxes(query_down_weight, 1, 2).reshape(low_cols, lane_width)
    value_down = jnp.swapaxes(value_down_weight, 1, 2).reshape(low_cols, lane_width)
    query_up = query_up_weight.reshape(low_cols, query_cols)
    value_up = value_up_weight.reshape(low_cols, kv_cols)

    def prepare(ids_ref, x_ref, *refs):
        out_refs, chosen_ids, part, sems = refs[:-3], refs[-3], refs[-2], refs[-1]
        me = lax.axis_index("adapter")
        lane = lax.axis_index("lane")
        lane_at = pl.ds(pl.multiple_of(lane * lane_width, lane_width), lane_width)
        copies = [
            pltpu.make_async_copy(ids_ref, chosen_ids, sems.at[owners_count]),
            pltpu.make_async_copy(x_ref.at[:, lane_at], part, sems.at[owners_count + 1]),
        ]
        for step in range(owners_count):
            other = jnp.bitwise_xor(me, step)
            at = pl.ds(pl.multiple_of(other * base_width, base_width), base_width)
            target = out_refs[step].at[:block_rows, :] if joined else out_refs[2 * step]
            copies.append(pltpu.make_async_copy(x_ref.at[:, at], target, sems.at[step]))
        for copy in copies:
            copy.start()
        copies[0].wait()
        owner = jnp.bitwise_xor(me, iota((slots, 1), 0) // capacity)
        chosen = slot_map(
            chosen_ids[...], owner, jnp.full((slots, 1), me), capacity, block_rows, nearby
        )
        fold = lax.rem(iota((rows, block_rows), 0), block_rows) == iota((rows, block_rows), 1)
        chosen = jnp.dot(
            chosen.astype(BF16), jnp.where(fold, 1.0, 0.0).astype(BF16), preferred_element_type=F32
        )
        copies[1].wait()
        placed = jnp.dot(chosen.astype(BF16), part[...], preferred_element_type=F32)
        for step in range(owners_count):
            mine = placed[step * capacity : (step + 1) * capacity].astype(BF16)
            if joined:
                out_refs[step][block_rows:, :] = mine
            else:
                out_refs[2 * step + 1][...] = mine
        for copy in copies[2:]:
            copy.wait()

    if joined:
        shapes = [jax.ShapeDtypeStruct((block_rows + capacity, base_width), BF16)] * owners_count
    else:
        shapes = [
            jax.ShapeDtypeStruct((block_rows, base_width), BF16),
            jax.ShapeDtypeStruct((capacity, lane_width), BF16),
        ] * owners_count
    sent = call(
        prepare, "prepare", shapes, [HBM] * 2, [VMEM] * len(shapes),
        (in_hbm(ids), in_hbm(residual_input)),
        scratch=[
            pltpu.VMEM((1, rows), jnp.int32),
            pltpu.VMEM((block_rows, lane_width), BF16),
            pltpu.SemaphoreType.DMA((owners_count + 2,)),
        ],
        moved=2**19,
    )
    per = len(sent) // owners_count
    arrived = [list(sent[:per])] + [None] * (owners_count - 1)
    for step in reversed(range(1, owners_count)):
        arrived[step] = [
            partner(piece, "adapter", step) for piece in sent[per * step : per * (step + 1)]
        ]
    arrived = sum(reversed(arrived), [])

    def fetch(arrays, name, after=None):
        def body(x_ref, *refs):
            refs = refs if after is None else refs[1:]
            sources, targets = refs[: len(arrays)], refs[len(arrays) : 2 * len(arrays)]
            sems = refs[-1]
            copies = [
                pltpu.make_async_copy(source, target, sems.at[i])
                for i, (source, target) in enumerate(zip(sources, targets))
            ]
            for copy in copies:
                copy.start()
            if after is not None:
                x = x_ref[...].astype(F32)
                mean = jnp.sum(x * x, axis=1, keepdims=True) * (1.0 / width)
                refs[-2][...] = jnp.broadcast_to(lax.rsqrt(mean + EPS), refs[-2].shape)
            for copy in copies:
                copy.wait()

        extra = [] if after is None else [jax.ShapeDtypeStruct((block_rows, 128), F32)]
        lead = [VMEM] if after is not None else [HBM]
        return call(
            body, name,
            [pltpu.VMEM(a.shape, a.dtype) for a in arrays] + extra,
            lead + ([] if after is None else [HBM]) + [HBM] * len(arrays),
            [VMEM] * (len(arrays) + len(extra)),
            (
                residual_input if after is not None else in_hbm(residual_input),
                *([] if after is None else [after]),
                *(in_hbm(a) for a in arrays),
            ),
            scratch=[pltpu.SemaphoreType.DMA((len(arrays),))],
            moved=sum(a.size * a.dtype.itemsize for a in arrays),
        )

    (w_query, w_key, w_value, w_query_down, w_value_down, w_query_up, w_value_up) = fetch(
        (query_weight, key_weight, value_weight, query_down, value_down, query_up, value_up),
        "fetch_weights",
    )

    def base_of(refs, step):
        at = owners_count - 1 - step
        return refs[at][:block_rows, :] if joined else refs[2 * at][...]

    def slots_of(refs, step):
        at = owners_count - 1 - step
        return refs[at][block_rows:, :] if joined else refs[2 * at + 1][...]

    def lower(gain_ref, dq_ref, dv_ref, *refs):
        part_refs, out_ref = refs[:-1], refs[-1]
        lane = lax.axis_index("lane")
        scaled = gain_ref[:, pl.ds(pl.multiple_of(lane * lane_width, lane_width), lane_width)]
        taken = jnp.concatenate(
            [slots_of(part_refs, step).astype(F32) for step in range(owners_count)], axis=0
        )
        taken = (taken * scaled).astype(BF16)
        contract = (((1,), (1,)), ((), ()))
        out_ref[:, :low_cols] = lax.dot_general(
            taken, dq_ref[...], contract, preferred_element_type=F32
        )
        out_ref[:, low_cols:] = lax.dot_general(
            taken, dv_ref[...], contract, preferred_element_type=F32
        )

    low = call(
        lower, "lower", jax.ShapeDtypeStruct((slots, 2 * low_cols), F32),
        [VMEM] * (3 + len(arrived)), VMEM, (gain, w_query_down, w_value_down, *arrived), moved=MIB,
    )
    lows = [low] + [partner(low, "lane", step) for step in range(1, lane_count)]

    def project(gain_ref, wq_ref, wk_ref, wv_ref, *refs):
        part_refs, out_ref, x_ref = refs[:-2], refs[-2], refs[-1]
        me = lax.axis_index("adapter")
        scaled = gain_ref[:, pl.ds(pl.multiple_of(me * base_width, base_width), base_width)]
        for step in range(owners_count):
            start = pl.multiple_of(jnp.bitwise_xor(me, step) * block_rows, block_rows)
            x_ref[pl.ds(start, block_rows), :] = (
                base_of(part_refs, step).astype(F32) * scaled
            ).astype(BF16)
        tile = min(1024, query_cols)
        for at in range(0, query_cols, tile):
            out_ref[:, at : at + tile] = jnp.dot(
                x_ref[...], wq_ref[:, at : at + tile], preferred_element_type=F32
            )
        out_ref[:, query_cols : query_cols + kv_cols] = jnp.dot(
            x_ref[...], wk_ref[...], preferred_element_type=F32
        )
        out_ref[:, query_cols + kv_cols :] = jnp.dot(
            x_ref[...], wv_ref[...], preferred_element_type=F32
        )

    based = call(
        project, "project", jax.ShapeDtypeStruct((rows, all_cols), F32),
        [VMEM] * (4 + len(arrived)), VMEM, (gain, w_query, w_key, w_value, *arrived),
        scratch=[pltpu.VMEM((rows, base_width), BF16)],
        flops=2 * rows * base_width * all_cols, moved=10 * MIB,
    )

    def raise_up(ids_ref, based_ref, uq_ref, uv_ref, *refs):
        low_refs, out_refs, sum_ref = refs[:lane_count], refs[lane_count:-1], refs[-1]
        me = lax.axis_index("adapter")
        block = jnp.bitwise_xor(me, iota((slots, 1), 0) // capacity)
        seen = slot_map(
            ids_ref[...], jnp.full((slots, 1), me), block, capacity, block_rows, nearby
        )
        total = low_refs[0][...]
        for ref in low_refs[1:]:
            total = total + ref[...]
        column = lax.rem(iota((slots, 2 * low_cols), 1) // rank, nearby)
        picked = jnp.zeros_like(total)
        for near in range(nearby):
            uses = jnp.where(ids_ref[...] == me * nearby + near, seen, 0.0)
            uses = jnp.sum(uses, axis=1, keepdims=True) > 0.5
            picked = jnp.where(uses & (column == near), total, picked)
        lowered = lax.dot_general(
            seen.astype(BF16), picked.astype(BF16), (((0,), (0,)), ((), ())),
            preferred_element_type=F32,
        ).astype(BF16)
        for at in range(0, query_cols, 1024):
            stop = min(at + 1024, query_cols)
            sum_ref[:, at:stop] = based_ref[:, at:stop] + ADAPTER_SCALE * jnp.dot(
                lowered[:, :low_cols], uq_ref[:, at:stop], preferred_element_type=F32
            )
        middle = slice(query_cols, query_cols + kv_cols)
        last = slice(query_cols + kv_cols, all_cols)
        sum_ref[:, middle] = based_ref[:, middle]
        sum_ref[:, last] = based_ref[:, last] + ADAPTER_SCALE * jnp.dot(
            lowered[:, low_cols:], uv_ref[...], preferred_element_type=F32
        )
        for step in range(owners_count):
            start = pl.multiple_of(jnp.bitwise_xor(me, step) * block_rows, block_rows)
            out_refs[step][...] = sum_ref[pl.ds(start, block_rows), :].astype(out_refs[step].dtype)

    parts = call(
        raise_up, "raise_up",
        [
            jax.ShapeDtypeStruct((block_rows, all_cols), BF16 if step else F32)
            for step in range(owners_count)
        ],
        [VMEM] * (4 + lane_count), [VMEM] * owners_count,
        (ids, based, w_query_up, w_value_up, *lows),
        scratch=[pltpu.VMEM((rows, all_cols), F32)],
    )
    keys, values, row_scale = fetch((cached_key_rows, cached_value_rows), "fetch_cache", parts[0])
    parts = [
        partner(parts[step], "adapter", step) for step in reversed(range(1, owners_count))
    ] + [parts[0]]

    def finish(length_ref, scale_ref, k_ref, v_ref, *refs):
        part_refs = refs[:owners_count]
        out_ref, fresh_ref, sum_ref, q_ref, s_ref, o_ref = refs[owners_count:]
        summed = part_refs[-1][...]
        for ref in part_refs[:-1]:
            summed = summed + ref[...].astype(F32)
        summed = (summed * scale_ref[:, :1]).astype(BF16)
        key_new = summed[:, query_cols : query_cols + kv_cols]
        value_new = summed[:, query_cols + kv_cols :]
        fresh_ref[...] = jnp.stack([key_new, value_new], axis=1)
        sum_ref[...] = summed.astype(F32)
        for head in range(heads):
            q_ref[:, head, :] = sum_ref[:, head * head_dim : (head + 1) * head_dim]
        scale = head_dim ** (-0.5)
        spot = iota((group_size, context), 1)
        own = []
        for row in range(block_rows):
            for group in range(kv_local):
                asked = q_ref[row, group * group_size : (group + 1) * group_size, :]
                scores = lax.dot_general(
                    asked.astype(BF16), k_ref[row, group], (((1,), (1,)), ((), ())),
                    preferred_element_type=F32,
                )
                s_ref[row * kv_local + group] = jnp.where(
                    spot < length_ref[row], scores * scale, -jnp.inf
                )
                at = query_cols + group * head_dim
                new = sum_ref[row : row + 1, at : at + head_dim]
                own.append(jnp.sum(asked * new, axis=1, keepdims=True))
        own_score = jnp.stack(own) * scale
        scores = s_ref[...]
        peak = jnp.maximum(jnp.max(scores, axis=2, keepdims=True), own_score)
        lifted = jnp.exp(scores - peak)
        own_lift = jnp.exp(own_score - peak)
        inverse = 1.0 / (jnp.sum(lifted, axis=2, keepdims=True) + own_lift)
        s_ref[...] = lifted * inverse
        own_weight = (own_lift * inverse).astype(BF16).astype(F32)
        for row in range(block_rows):
            for group in range(kv_local):
                index = row * kv_local + group
                mixed = jnp.dot(
                    s_ref[index].astype(BF16), v_ref[row, group], preferred_element_type=F32
                )
                at = query_cols + kv_cols + group * head_dim
                new = sum_ref[row : row + 1, at : at + head_dim]
                o_ref[row, group * group_size : (group + 1) * group_size, :] = (
                    mixed + own_weight[index] * new
                )
        for head in range(heads):
            out_ref[:, head * head_dim : (head + 1) * head_dim] = o_ref[:, head, :].astype(BF16)

    attended, fresh = call(
        finish, "finish",
        [
            jax.ShapeDtypeStruct((block_rows, query_cols), BF16),
            jax.ShapeDtypeStruct((block_rows, 2, kv_cols), BF16),
        ],
        [SMEM] + [VMEM] * (3 + owners_count), [VMEM] * 2,
        (cached_length, row_scale, keys, values, *parts),
        scratch=[
            pltpu.VMEM((block_rows, all_cols), F32),
            pltpu.VMEM((block_rows, heads, head_dim), F32),
            pltpu.VMEM((block_rows * kv_local, group_size, context), F32),
            pltpu.VMEM((block_rows, heads, head_dim), F32),
        ],
    )
    return (attended, fresh)


def solution(mesh):
    in_specs = (
        P(("groups", "adapter"), None),
        P(),
        P("adapter", "lane"),
        P("adapter", "lane"),
        P("adapter", "lane"),
        P("adapter", "lane", None),
        P("adapter", None, "lane"),
        P("adapter", "lane", None),
        P("adapter", None, "lane"),
        P(("groups", "adapter"), "lane", None, None),
        P(("groups", "adapter"), "lane", None, None),
        P("groups"),
        P(("groups", "adapter")),
    )
    out_specs = (P(("groups", "adapter"), "lane"), P(("groups", "adapter"), None, "lane"))
    return jax.shard_map(
        on_device, mesh=mesh, in_specs=in_specs, out_specs=out_specs, check_vma=False
    )
```

```python
import jax
import jax.numpy as jnp
from jax import lax
from jax.experimental import pallas as pl
from jax.experimental.pallas import tpu as pltpu
from jax.sharding import PartitionSpec as P

EPS = 1e-05
ADAPTER_SCALE = 0.5
MIB = 2**20
F32 = jnp.float32
BF16 = jnp.bfloat16
VMEM = pl.BlockSpec(memory_space=pltpu.VMEM)
SMEM = pl.BlockSpec(memory_space=pltpu.SMEM)
HBM = pl.BlockSpec(memory_space=pltpu.HBM)


def partner(array, axis, step):
    count = lax.axis_size(axis)
    return lax.ppermute(array, axis, [(i, i ^ step) for i in range(count)])


def call(body, name, outs, in_specs, out_specs, args, scratch=(), limit=16, flops=0, moved=0):
    return pl.pallas_call(
        body,
        name=name,
        out_shape=outs,
        in_specs=in_specs,
        out_specs=out_specs,
        scratch_shapes=scratch,
        compiler_params=pltpu.CompilerParams(vmem_limit_bytes=limit * MIB),
        cost_estimate=pl.CostEstimate(flops=flops, bytes_accessed=moved, transcendentals=0),
    )(*args)


def in_hbm(array):
    return pltpu.with_memory_space_constraint(array, pltpu.HBM)


def iota(shape, axis):
    return lax.broadcasted_iota(jnp.int32, shape, axis)


def slot_map(ids, owner, block, capacity, block_rows, nearby):
    slots, rows = owner.shape[0], ids.shape[1]
    first = owner * nearby
    spot = iota((slots, rows), 1)
    hit = (ids >= first) & (ids < first + nearby)
    hit = hit & (spot >= block * block_rows) & (spot < (block + 1) * block_rows)
    before = (iota((rows, rows), 0) < iota((rows, rows), 1)).astype(BF16)
    place = jnp.dot(
        jnp.where(hit, 1.0, 0.0).astype(BF16), before, preferred_element_type=F32
    )
    which = lax.rem(iota((slots, rows), 0), capacity).astype(F32)
    return jnp.where(hit & (place == which), 1.0, 0.0)


def on_device(
    residual_input,
    attention_norm_gain,
    query_weight,
    key_weight,
    value_weight,
    query_down_weight,
    query_up_weight,
    value_down_weight,
    value_up_weight,
    cached_key_rows,
    cached_value_rows,
    row_adapter_index,
    cached_length,
):
    owners_count = lax.axis_size("adapter")
    lane_count = lax.axis_size("lane")
    block_rows, width = residual_input.shape
    nearby, _, rank = query_down_weight.shape
    capacity = max(2, 2 * block_rows // owners_count)
    lane_width = width // lane_count
    base_width = width // owners_count
    query_cols = query_weight.shape[1]
    kv_cols = key_weight.shape[1]
    all_cols = query_cols + 2 * kv_cols
    slots = owners_count * capacity
    rows = owners_count * block_rows
    low_cols = nearby * rank
    half = base_width // 2
    joined = 2 * half == lane_width
    kv_local, context, head_dim = cached_key_rows.shape[1:]
    group_size = query_cols // head_dim // kv_local
    heads = kv_local * group_size

    ids = row_adapter_index.reshape(1, rows)
    gain = attention_norm_gain.reshape(1, width)
    query_down = jnp.swapaxes(query_down_weight, 1, 2).reshape(low_cols, lane_width)
    value_down = jnp.swapaxes(value_down_weight, 1, 2).reshape(low_cols, lane_width)
    query_up = query_up_weight.reshape(low_cols, query_cols)
    value_up = value_up_weight.reshape(low_cols, kv_cols)

    def prepare(ids_ref, x_ref, *refs):
        out_refs, chosen_ids, part, sems = refs[:-3], refs[-3], refs[-2], refs[-1]
        me = lax.axis_index("adapter")
        lane = lax.axis_index("lane")
        lane_at = pl.ds(pl.multiple_of(lane * lane_width, lane_width), lane_width)
        copies = [
            pltpu.make_async_copy(ids_ref, chosen_ids, sems.at[owners_count]),
            pltpu.make_async_copy(x_ref.at[:, lane_at], part, sems.at[owners_count + 1]),
        ]
        for step in range(owners_count):
            other = jnp.bitwise_xor(me, step)
            at = pl.ds(pl.multiple_of(other * base_width + lax.rem(lane, 2) * half, half), half)
            target = out_refs[step].at[:block_rows, :] if joined else out_refs[2 * step]
            copies.append(pltpu.make_async_copy(x_ref.at[:, at], target, sems.at[step]))
        for copy in copies:
            copy.start()
        copies[0].wait()
        owner = jnp.bitwise_xor(me, iota((slots, 1), 0) // capacity)
        chosen = slot_map(
            chosen_ids[...], owner, jnp.full((slots, 1), me), capacity, block_rows, nearby
        )
        fold = lax.rem(iota((rows, block_rows), 0), block_rows) == iota((rows, block_rows), 1)
        chosen = jnp.dot(
            chosen.astype(BF16), jnp.where(fold, 1.0, 0.0).astype(BF16), preferred_element_type=F32
        )
        copies[1].wait()
        placed = jnp.dot(chosen.astype(BF16), part[...], preferred_element_type=F32)
        for step in range(owners_count):
            mine = placed[step * capacity : (step + 1) * capacity]
            if joined:
                out_refs[step][block_rows:, :] = jnp.concatenate(
                    [mine[:, :half], mine[:, half:]], axis=0
                ).astype(BF16)
            else:
                out_refs[2 * step + 1][...] = mine.astype(BF16)
        for copy in copies[2:]:
            copy.wait()

    if joined:
        shapes = [jax.ShapeDtypeStruct((block_rows + 2 * capacity, half), BF16)] * owners_count
    else:
        shapes = [
            jax.ShapeDtypeStruct((block_rows, half), BF16),
            jax.ShapeDtypeStruct((capacity, lane_width), BF16),
        ] * owners_count
    sent = call(
        prepare, "prepare", shapes, [HBM] * 2, [VMEM] * len(shapes),
        (in_hbm(ids), in_hbm(residual_input)),
        scratch=[
            pltpu.VMEM((1, rows), jnp.int32),
            pltpu.VMEM((block_rows, lane_width), BF16),
            pltpu.SemaphoreType.DMA((owners_count + 2,)),
        ],
        moved=2**19,
    )
    per = len(sent) // owners_count
    arrived = [list(sent[:per])] + [None] * (owners_count - 1)
    for step in reversed(range(1, owners_count)):
        arrived[step] = [
            partner(piece, "adapter", step) for piece in sent[per * step : per * (step + 1)]
        ]
    arrived = sum(reversed(arrived), [])

    held = (query_weight, key_weight, value_weight, query_down, value_down, query_up, value_up)

    def fetch(x_ref, *refs):
        count = len(held)
        rms_ref, x_copy, sems = refs[2 * count :]
        copies = [pltpu.make_async_copy(x_ref, x_copy, sems.at[count])] + [
            pltpu.make_async_copy(refs[i], refs[count + i], sems.at[i]) for i in range(count)
        ]
        for copy in copies:
            copy.start()
        copies[0].wait()
        x = x_copy[...].astype(F32)
        mean = jnp.sum(x * x, axis=1, keepdims=True) * (1.0 / width)
        rms_ref[...] = jnp.broadcast_to(lax.rsqrt(mean + EPS), rms_ref.shape)
        for copy in copies[1:]:
            copy.wait()

    (w_query, w_key, w_value, w_query_down, w_value_down, w_query_up, w_value_up,
     row_scale) = call(
        fetch, "fetch",
        [pltpu.VMEM(a.shape, a.dtype) for a in held]
        + [jax.ShapeDtypeStruct((block_rows, 128), F32)],
        [HBM] * (1 + len(held)), [VMEM] * (1 + len(held)),
        (in_hbm(residual_input), *(in_hbm(a) for a in held)),
        scratch=[
            pltpu.VMEM((block_rows, width), BF16),
            pltpu.SemaphoreType.DMA((len(held) + 1,)),
        ],
        moved=sum(a.size * a.dtype.itemsize for a in held),
    )

    def base_of(refs, step):
        at = owners_count - 1 - step
        return refs[at][:block_rows, :] if joined else refs[2 * at][...]

    def slots_of(refs, step):
        at = owners_count - 1 - step
        if not joined:
            return refs[2 * at + 1][...].astype(F32)
        both = refs[at][block_rows:, :].astype(F32)
        return jnp.concatenate([both[:capacity], both[capacity:]], axis=1)

    def lower(gain_ref, dq_ref, dv_ref, *refs):
        part_refs, out_ref, half_ref = refs[:-2], refs[-2], refs[-1]
        lane = lax.axis_index("lane")
        scaled = gain_ref[:, pl.ds(pl.multiple_of(lane * lane_width, lane_width), lane_width)]
        taken = jnp.concatenate(
            [slots_of(part_refs, step) for step in range(owners_count)], axis=0
        )
        taken = (taken * scaled).astype(BF16)
        contract = (((1,), (1,)), ((), ()))
        out_ref[:, :low_cols] = lax.dot_general(
            taken, dq_ref[...], contract, preferred_element_type=F32
        )
        out_ref[:, low_cols:] = lax.dot_general(
            taken, dv_ref[...], contract, preferred_element_type=F32
        )
        me = lax.axis_index("adapter")
        first = me * base_width + lax.rem(lane, 2) * half
        scaled = gain_ref[:, pl.ds(pl.multiple_of(first, half), half)]
        for step in range(owners_count):
            start = pl.multiple_of(jnp.bitwise_xor(me, step) * block_rows, block_rows)
            half_ref[pl.ds(start, block_rows), :] = (
                base_of(part_refs, step).astype(F32) * scaled
            ).astype(BF16)

    low, near_half = call(
        lower, "lower",
        [
            jax.ShapeDtypeStruct((slots, 2 * low_cols), F32),
            jax.ShapeDtypeStruct((rows, half), BF16),
        ],
        [VMEM] * (3 + len(arrived)), [VMEM] * 2, (gain, w_query_down, w_value_down, *arrived),
        moved=MIB,
    )
    far_half = partner(near_half, "lane", 1)
    lows = [
        partner(low, "lane", step) for step in reversed(range(1, lane_count))
    ] + [low]

    def project(near_ref, far_ref, wq_ref, wk_ref, wv_ref, out_ref, x_ref):
        side = lax.rem(lax.axis_index("lane"), 2)
        x_ref[:, pl.ds(pl.multiple_of(side * half, half), half)] = near_ref[...]
        x_ref[:, pl.ds(pl.multiple_of((1 - side) * half, half), half)] = far_ref[...]
        tile = min(1024, query_cols)
        for at in range(0, query_cols, tile):
            out_ref[:, at : at + tile] = jnp.dot(
                x_ref[...], wq_ref[:, at : at + tile], preferred_element_type=F32
            )
        out_ref[:, query_cols : query_cols + kv_cols] = jnp.dot(
            x_ref[...], wk_ref[...], preferred_element_type=F32
        )
        out_ref[:, query_cols + kv_cols :] = jnp.dot(
            x_ref[...], wv_ref[...], preferred_element_type=F32
        )

    based = call(
        project, "project", jax.ShapeDtypeStruct((rows, all_cols), F32),
        [VMEM] * 5, VMEM, (near_half, far_half, w_query, w_key, w_value),
        scratch=[pltpu.VMEM((rows, base_width), BF16)],
        flops=2 * rows * base_width * all_cols, moved=10 * MIB,
    )

    def raise_up(ids_ref, based_ref, uq_ref, uv_ref, *refs):
        low_refs, out_refs, sum_ref = refs[:lane_count], refs[lane_count:-1], refs[-1]
        me = lax.axis_index("adapter")
        block = jnp.bitwise_xor(me, iota((slots, 1), 0) // capacity)
        seen = slot_map(
            ids_ref[...], jnp.full((slots, 1), me), block, capacity, block_rows, nearby
        )
        total = low_refs[0][...]
        for ref in low_refs[1:]:
            total = total + ref[...]
        column = lax.rem(iota((slots, 2 * low_cols), 1) // rank, nearby)
        picked = jnp.zeros_like(total)
        for near in range(nearby):
            uses = jnp.where(ids_ref[...] == me * nearby + near, seen, 0.0)
            uses = jnp.sum(uses, axis=1, keepdims=True) > 0.5
            picked = jnp.where(uses & (column == near), total, picked)
        lowered = lax.dot_general(
            seen.astype(BF16), picked.astype(BF16), (((0,), (0,)), ((), ())),
            preferred_element_type=F32,
        ).astype(BF16)
        for at in range(0, query_cols, 1024):
            stop = min(at + 1024, query_cols)
            sum_ref[:, at:stop] = based_ref[:, at:stop] + ADAPTER_SCALE * jnp.dot(
                lowered[:, :low_cols], uq_ref[:, at:stop], preferred_element_type=F32
            )
        middle = slice(query_cols, query_cols + kv_cols)
        last = slice(query_cols + kv_cols, all_cols)
        sum_ref[:, middle] = based_ref[:, middle]
        sum_ref[:, last] = based_ref[:, last] + ADAPTER_SCALE * jnp.dot(
            lowered[:, low_cols:], uv_ref[...], preferred_element_type=F32
        )
        for step in range(owners_count):
            start = pl.multiple_of(jnp.bitwise_xor(me, step) * block_rows, block_rows)
            out_refs[step][...] = sum_ref[pl.ds(start, block_rows), :].astype(out_refs[step].dtype)

    parts = call(
        raise_up, "raise_up",
        [
            jax.ShapeDtypeStruct((block_rows, all_cols), BF16 if step else F32)
            for step in range(owners_count)
        ],
        [VMEM] * (4 + lane_count), [VMEM] * owners_count,
        (ids, based, w_query_up, w_value_up, *lows),
        scratch=[pltpu.VMEM((rows, all_cols), F32)],
    )
    parts = [
        partner(parts[step], "adapter", step) for step in reversed(range(1, owners_count))
    ] + [parts[0]]

    def finish(length_ref, scale_ref, k_ref, v_ref, *refs):
        part_refs = refs[:owners_count]
        out_ref, fresh_ref, sum_ref, q_ref, s_ref, o_ref = refs[owners_count:]
        summed = part_refs[-1][...]
        for ref in part_refs[:-1]:
            summed = summed + ref[...].astype(F32)
        summed = (summed * scale_ref[:, :1]).astype(BF16)
        key_new = summed[:, query_cols : query_cols + kv_cols]
        value_new = summed[:, query_cols + kv_cols :]
        fresh_ref[...] = jnp.stack([key_new, value_new], axis=1)
        sum_ref[...] = summed.astype(F32)
        for head in range(heads):
            q_ref[:, head, :] = sum_ref[:, head * head_dim : (head + 1) * head_dim]
        scale = head_dim ** (-0.5)
        spot = iota((group_size, context), 1)
        own = []
        for row in range(block_rows):
            for group in range(kv_local):
                asked = q_ref[row, group * group_size : (group + 1) * group_size, :]
                scores = lax.dot_general(
                    asked.astype(BF16), k_ref[row, group], (((1,), (1,)), ((), ())),
                    preferred_element_type=F32,
                )
                s_ref[row * kv_local + group] = jnp.where(
                    spot < length_ref[row], scores * scale, -jnp.inf
                )
                at = query_cols + group * head_dim
                new = sum_ref[row : row + 1, at : at + head_dim]
                own.append(jnp.sum(asked * new, axis=1, keepdims=True))
        own_score = jnp.stack(own) * scale
        scores = s_ref[...]
        peak = jnp.maximum(jnp.max(scores, axis=2, keepdims=True), own_score)
        lifted = jnp.exp(scores - peak)
        own_lift = jnp.exp(own_score - peak)
        inverse = 1.0 / (jnp.sum(lifted, axis=2, keepdims=True) + own_lift)
        s_ref[...] = lifted * inverse
        own_weight = (own_lift * inverse).astype(BF16).astype(F32)
        for row in range(block_rows):
            for group in range(kv_local):
                index = row * kv_local + group
                mixed = jnp.dot(
                    s_ref[index].astype(BF16), v_ref[row, group], preferred_element_type=F32
                )
                at = query_cols + kv_cols + group * head_dim
                new = sum_ref[row : row + 1, at : at + head_dim]
                o_ref[row, group * group_size : (group + 1) * group_size, :] = (
                    mixed + own_weight[index] * new
                )
        for head in range(heads):
            out_ref[:, head * head_dim : (head + 1) * head_dim] = o_ref[:, head, :].astype(BF16)

    attended, fresh = call(
        finish, "finish",
        [
            jax.ShapeDtypeStruct((block_rows, query_cols), BF16),
            jax.ShapeDtypeStruct((block_rows, 2, kv_cols), BF16),
        ],
        [SMEM] + [VMEM] * (3 + owners_count), [VMEM] * 2,
        (cached_length, row_scale, cached_key_rows, cached_value_rows, *parts),
        scratch=[
            pltpu.VMEM((block_rows, all_cols), F32),
            pltpu.VMEM((block_rows, heads, head_dim), F32),
            pltpu.VMEM((block_rows * kv_local, group_size, context), F32),
            pltpu.VMEM((block_rows, heads, head_dim), F32),
        ],
    )
    return (attended, fresh)


def solution(mesh):
    in_specs = (
        P(("groups", "adapter"), None),
        P(),
        P("adapter", "lane"),
        P("adapter", "lane"),
        P("adapter", "lane"),
        P("adapter", "lane", None),
        P("adapter", None, "lane"),
        P("adapter", "lane", None),
        P("adapter", None, "lane"),
        P(("groups", "adapter"), "lane", None, None),
        P(("groups", "adapter"), "lane", None, None),
        P("groups"),
        P(("groups", "adapter")),
    )
    out_specs = (P(("groups", "adapter"), "lane"), P(("groups", "adapter"), None, "lane"))
    return jax.shard_map(
        on_device, mesh=mesh, in_specs=in_specs, out_specs=out_specs, check_vma=False
    )
```

```python
import jax
import jax.numpy as jnp
from jax import lax
from jax.experimental import pallas as pl
from jax.experimental.pallas import tpu as pltpu
from jax.sharding import PartitionSpec as P

EPS = 1e-05
ADAPTER_SCALE = 0.5
MIB = 2**20
F32 = jnp.float32
BF16 = jnp.bfloat16
VMEM = pl.BlockSpec(memory_space=pltpu.VMEM)
SMEM = pl.BlockSpec(memory_space=pltpu.SMEM)
HBM = pl.BlockSpec(memory_space=pltpu.HBM)


def partner(array, axis, step):
    count = lax.axis_size(axis)
    return lax.ppermute(array, axis, [(i, i ^ step) for i in range(count)])


def call(body, name, outs, in_specs, out_specs, args, scratch=(), limit=16, flops=0, moved=0):
    return pl.pallas_call(
        body,
        name=name,
        out_shape=outs,
        in_specs=in_specs,
        out_specs=out_specs,
        scratch_shapes=scratch,
        compiler_params=pltpu.CompilerParams(vmem_limit_bytes=limit * MIB),
        cost_estimate=pl.CostEstimate(flops=flops, bytes_accessed=moved, transcendentals=0),
    )(*args)


def in_hbm(array):
    return pltpu.with_memory_space_constraint(array, pltpu.HBM)


def iota(shape, axis):
    return lax.broadcasted_iota(jnp.int32, shape, axis)


def slot_map(ids, owner, block, capacity, block_rows, nearby):
    slots, rows = owner.shape[0], ids.shape[1]
    first = owner * nearby
    spot = iota((slots, rows), 1)
    hit = (ids >= first) & (ids < first + nearby)
    hit = hit & (spot >= block * block_rows) & (spot < (block + 1) * block_rows)
    before = (iota((rows, rows), 0) < iota((rows, rows), 1)).astype(BF16)
    place = jnp.dot(
        jnp.where(hit, 1.0, 0.0).astype(BF16), before, preferred_element_type=F32
    )
    which = lax.rem(iota((slots, rows), 0), capacity).astype(F32)
    return jnp.where(hit & (place == which), 1.0, 0.0)


def on_device(
    residual_input,
    attention_norm_gain,
    query_weight,
    key_weight,
    value_weight,
    query_down_weight,
    query_up_weight,
    value_down_weight,
    value_up_weight,
    cached_key_rows,
    cached_value_rows,
    row_adapter_index,
    cached_length,
):
    owners_count = lax.axis_size("adapter")
    lane_count = lax.axis_size("lane")
    block_rows, width = residual_input.shape
    nearby, _, rank = query_down_weight.shape
    capacity = max(2, 2 * block_rows // owners_count)
    lane_width = width // lane_count
    base_width = width // owners_count
    query_cols = query_weight.shape[1]
    kv_cols = key_weight.shape[1]
    all_cols = query_cols + 2 * kv_cols
    slots = owners_count * capacity
    rows = owners_count * block_rows
    low_cols = nearby * rank
    half = base_width // 2
    joined = 2 * half == lane_width
    kv_local, context, head_dim = cached_key_rows.shape[1:]
    group_size = query_cols // head_dim // kv_local
    heads = kv_local * group_size

    ids = row_adapter_index.reshape(1, rows)
    gain = attention_norm_gain.reshape(1, width)
    query_down = jnp.swapaxes(query_down_weight, 1, 2).reshape(low_cols, lane_width)
    value_down = jnp.swapaxes(value_down_weight, 1, 2).reshape(low_cols, lane_width)
    query_up = query_up_weight.reshape(low_cols, query_cols)
    value_up = value_up_weight.reshape(low_cols, kv_cols)

    def prepare(ids_ref, x_ref, *refs):
        out_refs, chosen_ids, part, sems = refs[:-3], refs[-3], refs[-2], refs[-1]
        me = lax.axis_index("adapter")
        lane = lax.axis_index("lane")
        lane_at = pl.ds(pl.multiple_of(lane * lane_width, lane_width), lane_width)
        copies = [
            pltpu.make_async_copy(ids_ref, chosen_ids, sems.at[owners_count]),
            pltpu.make_async_copy(x_ref.at[:, lane_at], part, sems.at[owners_count + 1]),
        ]
        for step in range(owners_count):
            other = jnp.bitwise_xor(me, step)
            at = pl.ds(pl.multiple_of(other * base_width + lax.rem(lane, 2) * half, half), half)
            target = out_refs[step].at[:block_rows, :] if joined else out_refs[2 * step]
            copies.append(pltpu.make_async_copy(x_ref.at[:, at], target, sems.at[step]))
        for copy in copies:
            copy.start()
        copies[0].wait()
        owner = jnp.bitwise_xor(me, iota((slots, 1), 0) // capacity)
        chosen = slot_map(
            chosen_ids[...], owner, jnp.full((slots, 1), me), capacity, block_rows, nearby
        )
        fold = lax.rem(iota((rows, block_rows), 0), block_rows) == iota((rows, block_rows), 1)
        chosen = jnp.dot(
            chosen.astype(BF16), jnp.where(fold, 1.0, 0.0).astype(BF16), preferred_element_type=F32
        )
        copies[1].wait()
        placed = jnp.dot(chosen.astype(BF16), part[...], preferred_element_type=F32)
        for step in range(owners_count):
            mine = placed[step * capacity : (step + 1) * capacity]
            if joined:
                out_refs[step][block_rows:, :] = jnp.concatenate(
                    [mine[:, :half], mine[:, half:]], axis=0
                ).astype(BF16)
            else:
                out_refs[2 * step + 1][...] = mine.astype(BF16)
        for copy in copies[2:]:
            copy.wait()

    if joined:
        shapes = [jax.ShapeDtypeStruct((block_rows + 2 * capacity, half), BF16)] * owners_count
    else:
        shapes = [
            jax.ShapeDtypeStruct((block_rows, half), BF16),
            jax.ShapeDtypeStruct((capacity, lane_width), BF16),
        ] * owners_count
    sent = call(
        prepare, "prepare", shapes, [HBM] * 2, [VMEM] * len(shapes),
        (in_hbm(ids), in_hbm(residual_input)),
        scratch=[
            pltpu.VMEM((1, rows), jnp.int32),
            pltpu.VMEM((block_rows, lane_width), BF16),
            pltpu.SemaphoreType.DMA((owners_count + 2,)),
        ],
        moved=2**19,
    )
    per = len(sent) // owners_count
    arrived = [list(sent[:per])] + [None] * (owners_count - 1)
    for step in reversed(range(1, owners_count)):
        arrived[step] = [
            partner(piece, "adapter", step) for piece in sent[per * step : per * (step + 1)]
        ]
    arrived = sum(reversed(arrived), [])

    held = (query_down, value_down, query_weight, key_weight, value_weight)

    def survey(ids_ref, x_ref, *refs):
        count = len(held)
        rms_ref, seen_ref, mask_ref, ids_copy, x_copy, sems = refs[2 * count :]
        copies = [
            pltpu.make_async_copy(ids_ref, ids_copy, sems.at[0]),
            pltpu.make_async_copy(x_ref, x_copy, sems.at[1]),
        ] + [
            pltpu.make_async_copy(refs[i], refs[count + i], sems.at[2 + i]) for i in range(count)
        ]
        for copy in copies:
            copy.start()
        copies[0].wait()
        me = lax.axis_index("adapter")
        block = jnp.bitwise_xor(me, iota((slots, 1), 0) // capacity)
        seen = slot_map(
            ids_copy[...], jnp.full((slots, 1), me), block, capacity, block_rows, nearby
        )
        seen_ref[...] = seen.astype(BF16)
        column = lax.rem(iota((slots, 2 * low_cols), 1) // rank, nearby)
        mask = jnp.zeros((slots, 2 * low_cols), F32)
        for near in range(nearby):
            uses = jnp.where(ids_copy[...] == me * nearby + near, seen, 0.0)
            uses = jnp.sum(uses, axis=1, keepdims=True)
            mask = jnp.where(column == near, uses, mask)
        mask_ref[...] = mask
        copies[1].wait()
        x = x_copy[...].astype(F32)
        mean = jnp.sum(x * x, axis=1, keepdims=True) * (1.0 / width)
        rms_ref[...] = jnp.broadcast_to(lax.rsqrt(mean + EPS), rms_ref.shape)
        for copy in copies[2:]:
            copy.wait()

    (w_query_down, w_value_down, w_query, w_key, w_value, row_scale, seen, mask) = call(
        survey, "survey",
        [pltpu.VMEM(a.shape, a.dtype) for a in held]
        + [
            jax.ShapeDtypeStruct((block_rows, 128), F32),
            jax.ShapeDtypeStruct((slots, rows), BF16),
            jax.ShapeDtypeStruct((slots, 2 * low_cols), F32),
        ],
        [HBM] * (2 + len(held)), [VMEM] * (3 + len(held)),
        (in_hbm(ids), in_hbm(residual_input), *(in_hbm(a) for a in held)),
        scratch=[
            pltpu.VMEM((1, rows), jnp.int32),
            pltpu.VMEM((block_rows, width), BF16),
            pltpu.SemaphoreType.DMA((2 + len(held),)),
        ],
        moved=12 * MIB,
    )

    def base_of(refs, step):
        at = owners_count - 1 - step
        return refs[at][:block_rows, :] if joined else refs[2 * at][...]

    def slots_of(refs, step):
        at = owners_count - 1 - step
        if not joined:
            return refs[2 * at + 1][...].astype(F32)
        both = refs[at][block_rows:, :].astype(F32)
        return jnp.concatenate([both[:capacity], both[capacity:]], axis=1)

    def lower(gain_ref, mask_ref, dq_ref, dv_ref, *refs):
        part_refs, out_ref, half_ref = refs[:-2], refs[-2], refs[-1]
        lane = lax.axis_index("lane")
        scaled = gain_ref[:, pl.ds(pl.multiple_of(lane * lane_width, lane_width), lane_width)]
        taken = jnp.concatenate(
            [slots_of(part_refs, step) for step in range(owners_count)], axis=0
        )
        taken = (taken * scaled).astype(BF16)
        contract = (((1,), (1,)), ((), ()))
        for at, ref in enumerate((dq_ref, dv_ref)):
            every = mask_ref[:, at * low_cols : (at + 1) * low_cols] * lax.dot_general(
                taken, ref[...], contract, preferred_element_type=F32
            )
            picked = every[:, :rank]
            for near in range(1, nearby):
                picked = picked + every[:, near * rank : (near + 1) * rank]
            out_ref[:, at * rank : (at + 1) * rank] = picked
        me = lax.axis_index("adapter")
        first = me * base_width + lax.rem(lane, 2) * half
        scaled = gain_ref[:, pl.ds(pl.multiple_of(first, half), half)]
        for step in range(owners_count):
            start = pl.multiple_of(jnp.bitwise_xor(me, step) * block_rows, block_rows)
            half_ref[pl.ds(start, block_rows), :] = (
                base_of(part_refs, step).astype(F32) * scaled
            ).astype(BF16)

    low, near_half = call(
        lower, "lower",
        [
            jax.ShapeDtypeStruct((slots, 2 * rank), F32),
            jax.ShapeDtypeStruct((rows, half), BF16),
        ],
        [VMEM] * (4 + len(arrived)), [VMEM] * 2,
        (gain, mask, w_query_down, w_value_down, *arrived),
        moved=MIB,
    )
    far_half = partner(near_half, "lane", 1)
    lows = [low] + [partner(low, "lane", step) for step in range(1, lane_count)]

    def project(near_ref, far_ref, wq_ref, wk_ref, wv_ref, out_ref, x_ref):
        side = lax.rem(lax.axis_index("lane"), 2)
        x_ref[:, pl.ds(pl.multiple_of(side * half, half), half)] = near_ref[...]
        x_ref[:, pl.ds(pl.multiple_of((1 - side) * half, half), half)] = far_ref[...]
        tile = min(1024, query_cols)
        for at in range(0, query_cols, tile):
            out_ref[:, at : at + tile] = jnp.dot(
                x_ref[...], wq_ref[:, at : at + tile], preferred_element_type=F32
            )
        out_ref[:, query_cols : query_cols + kv_cols] = jnp.dot(
            x_ref[...], wk_ref[...], preferred_element_type=F32
        )
        out_ref[:, query_cols + kv_cols :] = jnp.dot(
            x_ref[...], wv_ref[...], preferred_element_type=F32
        )

    based = call(
        project, "project", jax.ShapeDtypeStruct((rows, all_cols), F32),
        [VMEM] * 5, VMEM, (near_half, far_half, w_query, w_key, w_value),
        scratch=[pltpu.VMEM((rows, base_width), BF16)],
        flops=2 * rows * base_width * all_cols, moved=10 * MIB,
    )

    def raise_up(seen_ref, mask_ref, based_ref, uq_ref, uv_ref, *refs):
        low_refs, out_refs, sum_ref = refs[:lane_count], refs[lane_count:-1], refs[-1]
        me = lax.axis_index("adapter")
        total = low_refs[0][...]
        for ref in low_refs[1:]:
            total = total + ref[...]
        spread = [total[:, :rank]] * nearby + [total[:, rank:]] * nearby
        spread = jnp.concatenate(spread, axis=1) * mask_ref[...]
        lowered = lax.dot_general(
            seen_ref[...], spread.astype(BF16), (((0,), (0,)), ((), ())),
            preferred_element_type=F32,
        ).astype(BF16)
        for at in range(0, query_cols, 1024):
            stop = min(at + 1024, query_cols)
            sum_ref[:, at:stop] = based_ref[:, at:stop] + ADAPTER_SCALE * jnp.dot(
                lowered[:, :low_cols], uq_ref[:, at:stop], preferred_element_type=F32
            )
        middle = slice(query_cols, query_cols + kv_cols)
        last = slice(query_cols + kv_cols, all_cols)
        sum_ref[:, middle] = based_ref[:, middle]
        sum_ref[:, last] = based_ref[:, last] + ADAPTER_SCALE * jnp.dot(
            lowered[:, low_cols:], uv_ref[...], preferred_element_type=F32
        )
        for step in range(owners_count):
            start = pl.multiple_of(jnp.bitwise_xor(me, step) * block_rows, block_rows)
            out_refs[step][...] = sum_ref[pl.ds(start, block_rows), :].astype(out_refs[step].dtype)

    parts = call(
        raise_up, "raise_up",
        [
            jax.ShapeDtypeStruct((block_rows, all_cols), BF16 if step else F32)
            for step in range(owners_count)
        ],
        [VMEM] * (5 + lane_count), [VMEM] * owners_count,
        (seen, mask, based, query_up, value_up, *lows),
        scratch=[pltpu.VMEM((rows, all_cols), F32)],
    )
    parts = [
        partner(parts[step], "adapter", step) for step in reversed(range(1, owners_count))
    ] + [parts[0]]

    def finish(length_ref, scale_ref, k_ref, v_ref, *refs):
        part_refs = refs[:owners_count]
        out_ref, fresh_ref, sum_ref, q_ref, s_ref, o_ref = refs[owners_count:]
        summed = part_refs[-1][...]
        for ref in part_refs[:-1]:
            summed = summed + ref[...].astype(F32)
        summed = (summed * scale_ref[:, :1]).astype(BF16)
        key_new = summed[:, query_cols : query_cols + kv_cols]
        value_new = summed[:, query_cols + kv_cols :]
        fresh_ref[...] = jnp.stack([key_new, value_new], axis=1)
        sum_ref[...] = summed.astype(F32)
        for head in range(heads):
            q_ref[:, head, :] = sum_ref[:, head * head_dim : (head + 1) * head_dim]
        scale = head_dim ** (-0.5)
        spot = iota((group_size, context), 1)
        own = []
        for row in range(block_rows):
            for group in range(kv_local):
                asked = q_ref[row, group * group_size : (group + 1) * group_size, :]
                scores = lax.dot_general(
                    asked.astype(BF16), k_ref[row, group], (((1,), (1,)), ((), ())),
                    preferred_element_type=F32,
                )
                s_ref[row * kv_local + group] = jnp.where(
                    spot < length_ref[row], scores * scale, -jnp.inf
                )
                at = query_cols + group * head_dim
                new = sum_ref[row : row + 1, at : at + head_dim]
                own.append(jnp.sum(asked * new, axis=1, keepdims=True))
        own_score = jnp.stack(own) * scale
        scores = s_ref[...]
        peak = jnp.maximum(jnp.max(scores, axis=2, keepdims=True), own_score)
        lifted = jnp.exp(scores - peak)
        own_lift = jnp.exp(own_score - peak)
        inverse = 1.0 / (jnp.sum(lifted, axis=2, keepdims=True) + own_lift)
        s_ref[...] = lifted * inverse
        own_weight = (own_lift * inverse).astype(BF16).astype(F32)
        for row in range(block_rows):
            for group in range(kv_local):
                index = row * kv_local + group
                mixed = jnp.dot(
                    s_ref[index].astype(BF16), v_ref[row, group], preferred_element_type=F32
                )
                at = query_cols + kv_cols + group * head_dim
                new = sum_ref[row : row + 1, at : at + head_dim]
                o_ref[row, group * group_size : (group + 1) * group_size, :] = (
                    mixed + own_weight[index] * new
                )
        for head in range(heads):
            out_ref[:, head * head_dim : (head + 1) * head_dim] = o_ref[:, head, :].astype(BF16)

    attended, fresh = call(
        finish, "finish",
        [
            jax.ShapeDtypeStruct((block_rows, query_cols), BF16),
            jax.ShapeDtypeStruct((block_rows, 2, kv_cols), BF16),
        ],
        [SMEM] + [VMEM] * (3 + owners_count), [VMEM] * 2,
        (cached_length, row_scale, cached_key_rows, cached_value_rows, *parts),
        scratch=[
            pltpu.VMEM((block_rows, all_cols), F32),
            pltpu.VMEM((block_rows, heads, head_dim), F32),
            pltpu.VMEM((block_rows * kv_local, group_size, context), F32),
            pltpu.VMEM((block_rows, heads, head_dim), F32),
        ],
    )
    return (attended, fresh)


def solution(mesh):
    in_specs = (
        P(("groups", "adapter"), None),
        P(),
        P("adapter", "lane"),
        P("adapter", "lane"),
        P("adapter", "lane"),
        P("adapter", "lane", None),
        P("adapter", None, "lane"),
        P("adapter", "lane", None),
        P("adapter", None, "lane"),
        P(("groups", "adapter"), "lane", None, None),
        P(("groups", "adapter"), "lane", None, None),
        P("groups"),
        P(("groups", "adapter")),
    )
    out_specs = (P(("groups", "adapter"), "lane"), P(("groups", "adapter"), None, "lane"))
    return jax.shard_map(
        on_device, mesh=mesh, in_specs=in_specs, out_specs=out_specs, check_vma=False
    )
```

```python
import jax
import jax.numpy as jnp
from jax import lax
from jax.experimental import pallas as pl
from jax.experimental.pallas import tpu as pltpu
from jax.sharding import PartitionSpec as P

EPS = 1e-05
ADAPTER_SCALE = 0.5
MIB = 2**20
F32 = jnp.float32
BF16 = jnp.bfloat16
VMEM = pl.BlockSpec(memory_space=pltpu.VMEM)
HBM = pl.BlockSpec(memory_space=pltpu.HBM)


def partner(array, axis, step):
    count = lax.axis_size(axis)
    return lax.ppermute(array, axis, [(i, i ^ step) for i in range(count)])


def call(body, name, outs, in_specs, out_specs, args, scratch=(), limit=16, flops=0, moved=0):
    return pl.pallas_call(
        body,
        name=name,
        out_shape=outs,
        in_specs=in_specs,
        out_specs=out_specs,
        scratch_shapes=scratch,
        compiler_params=pltpu.CompilerParams(vmem_limit_bytes=limit * MIB),
        cost_estimate=pl.CostEstimate(flops=flops, bytes_accessed=moved, transcendentals=0),
    )(*args)


def in_hbm(array):
    return pltpu.with_memory_space_constraint(array, pltpu.HBM)


def iota(shape, axis):
    return lax.broadcasted_iota(jnp.int32, shape, axis)


def slot_map(ids, owner, block, capacity, block_rows, nearby):
    slots, rows = owner.shape[0], ids.shape[1]
    first = owner * nearby
    spot = iota((slots, rows), 1)
    hit = (ids >= first) & (ids < first + nearby)
    hit = hit & (spot >= block * block_rows) & (spot < (block + 1) * block_rows)
    before = (iota((rows, rows), 0) < iota((rows, rows), 1)).astype(BF16)
    place = jnp.dot(
        jnp.where(hit, 1.0, 0.0).astype(BF16), before, preferred_element_type=F32
    )
    which = lax.rem(iota((slots, rows), 0), capacity).astype(F32)
    return jnp.where(hit & (place == which), 1.0, 0.0)


def on_device(
    residual_input,
    attention_norm_gain,
    query_weight,
    key_weight,
    value_weight,
    query_down_weight,
    query_up_weight,
    value_down_weight,
    value_up_weight,
    cached_key_rows,
    cached_value_rows,
    row_adapter_index,
    cached_length,
):
    owners_count = lax.axis_size("adapter")
    lane_count = lax.axis_size("lane")
    block_rows, width = residual_input.shape
    nearby, _, rank = query_down_weight.shape
    capacity = max(2, 2 * block_rows // owners_count)
    lane_width = width // lane_count
    base_width = width // owners_count
    query_cols = query_weight.shape[1]
    kv_cols = key_weight.shape[1]
    all_cols = query_cols + 2 * kv_cols
    slots = owners_count * capacity
    rows = owners_count * block_rows
    low_cols = nearby * rank
    half = base_width // 2
    joined = 2 * half == lane_width
    kv_local, context, head_dim = cached_key_rows.shape[1:]
    group_size = query_cols // head_dim // kv_local
    heads = kv_local * group_size

    ids = row_adapter_index.reshape(1, rows)
    gain = attention_norm_gain.reshape(1, width)
    query_down = jnp.swapaxes(query_down_weight, 1, 2).reshape(low_cols, lane_width)
    value_down = jnp.swapaxes(value_down_weight, 1, 2).reshape(low_cols, lane_width)
    query_up = query_up_weight.reshape(low_cols, query_cols)
    value_up = value_up_weight.reshape(low_cols, kv_cols)

    def prepare(ids_ref, x_ref, *refs):
        out_refs, chosen_ids, part, sems = refs[:-3], refs[-3], refs[-2], refs[-1]
        me = lax.axis_index("adapter")
        lane = lax.axis_index("lane")
        lane_at = pl.ds(pl.multiple_of(lane * lane_width, lane_width), lane_width)
        copies = [
            pltpu.make_async_copy(ids_ref, chosen_ids, sems.at[owners_count]),
            pltpu.make_async_copy(x_ref.at[:, lane_at], part, sems.at[owners_count + 1]),
        ]
        for step in range(owners_count):
            other = jnp.bitwise_xor(me, step)
            at = pl.ds(pl.multiple_of(other * base_width + lax.rem(lane, 2) * half, half), half)
            target = out_refs[step].at[:block_rows, :] if joined else out_refs[2 * step]
            copies.append(pltpu.make_async_copy(x_ref.at[:, at], target, sems.at[step]))
        for copy in copies:
            copy.start()
        copies[0].wait()
        owner = jnp.bitwise_xor(me, iota((slots, 1), 0) // capacity)
        chosen = slot_map(
            chosen_ids[...], owner, jnp.full((slots, 1), me), capacity, block_rows, nearby
        )
        fold = lax.rem(iota((rows, block_rows), 0), block_rows) == iota((rows, block_rows), 1)
        chosen = jnp.dot(
            chosen.astype(BF16), jnp.where(fold, 1.0, 0.0).astype(BF16), preferred_element_type=F32
        )
        copies[1].wait()
        placed = jnp.dot(chosen.astype(BF16), part[...], preferred_element_type=F32)
        for step in range(owners_count):
            mine = placed[step * capacity : (step + 1) * capacity]
            if joined:
                out_refs[step][block_rows:, :] = jnp.concatenate(
                    [mine[:, :half], mine[:, half:]], axis=0
                ).astype(BF16)
            else:
                out_refs[2 * step + 1][...] = mine.astype(BF16)
        for copy in copies[2:]:
            copy.wait()

    if joined:
        shapes = [jax.ShapeDtypeStruct((block_rows + 2 * capacity, half), BF16)] * owners_count
    else:
        shapes = [
            jax.ShapeDtypeStruct((block_rows, half), BF16),
            jax.ShapeDtypeStruct((capacity, lane_width), BF16),
        ] * owners_count
    sent = call(
        prepare, "prepare", shapes, [HBM] * 2, [VMEM] * len(shapes),
        (in_hbm(ids), in_hbm(residual_input)),
        scratch=[
            pltpu.VMEM((1, rows), jnp.int32),
            pltpu.VMEM((block_rows, lane_width), BF16),
            pltpu.SemaphoreType.DMA((owners_count + 2,)),
        ],
        moved=2**19,
    )
    per = len(sent) // owners_count
    arrived = [list(sent[:per])] + [None] * (owners_count - 1)
    for step in reversed(range(1, owners_count)):
        arrived[step] = [
            partner(piece, "adapter", step) for piece in sent[per * step : per * (step + 1)]
        ]
    arrived = sum(reversed(arrived), [])

    held = (query_down, value_down, query_weight, key_weight, value_weight)

    def survey(ids_ref, x_ref, length_ref, *refs):
        count = len(held)
        rms_ref, seen_ref, mask_ref, many_ref, ids_copy, x_copy, length_copy, sems = refs[2 * count :]
        copies = [
            pltpu.make_async_copy(ids_ref, ids_copy, sems.at[0]),
            pltpu.make_async_copy(x_ref, x_copy, sems.at[1]),
            pltpu.make_async_copy(length_ref, length_copy, sems.at[2]),
        ] + [
            pltpu.make_async_copy(refs[i], refs[count + i], sems.at[3 + i]) for i in range(count)
        ]
        for copy in copies:
            copy.start()
        copies[0].wait()
        me = lax.axis_index("adapter")
        block = jnp.bitwise_xor(me, iota((slots, 1), 0) // capacity)
        seen = slot_map(
            ids_copy[...], jnp.full((slots, 1), me), block, capacity, block_rows, nearby
        )
        seen_ref[...] = seen.astype(BF16)
        column = lax.rem(iota((slots, 2 * low_cols), 1) // rank, nearby)
        mask = jnp.zeros((slots, 2 * low_cols), F32)
        for near in range(nearby):
            uses = jnp.where(ids_copy[...] == me * nearby + near, seen, 0.0)
            uses = jnp.sum(uses, axis=1, keepdims=True)
            mask = jnp.where(column == near, uses, mask)
        mask_ref[...] = mask
        copies[2].wait()
        same = iota((block_rows, block_rows), 0) == iota((block_rows, block_rows), 1)
        many = jnp.sum(
            jnp.where(same, length_copy[...].astype(F32), 0.0), axis=1, keepdims=True
        )
        many_ref[...] = jnp.broadcast_to(many, many_ref.shape)
        copies[1].wait()
        x = x_copy[...].astype(F32)
        mean = jnp.sum(x * x, axis=1, keepdims=True) * (1.0 / width)
        rms_ref[...] = jnp.broadcast_to(lax.rsqrt(mean + EPS), rms_ref.shape)
        for copy in copies[3:]:
            copy.wait()

    (w_query_down, w_value_down, w_query, w_key, w_value, row_scale, seen, mask,
     row_length) = call(
        survey, "survey",
        [pltpu.VMEM(a.shape, a.dtype) for a in held]
        + [
            jax.ShapeDtypeStruct((block_rows, 128), F32),
            jax.ShapeDtypeStruct((slots, rows), BF16),
            jax.ShapeDtypeStruct((slots, 2 * low_cols), F32),
            jax.ShapeDtypeStruct((block_rows, context), F32),
        ],
        [HBM] * (3 + len(held)), [VMEM] * (4 + len(held)),
        (in_hbm(ids), in_hbm(residual_input), in_hbm(cached_length.reshape(1, block_rows)),
         *(in_hbm(a) for a in held)),
        scratch=[
            pltpu.VMEM((1, rows), jnp.int32),
            pltpu.VMEM((block_rows, width), BF16),
            pltpu.VMEM((1, block_rows), jnp.int32),
            pltpu.SemaphoreType.DMA((3 + len(held),)),
        ],
        moved=12 * MIB,
    )

    def base_of(refs, step):
        at = owners_count - 1 - step
        return refs[at][:block_rows, :] if joined else refs[2 * at][...]

    def slots_of(refs, step):
        at = owners_count - 1 - step
        if not joined:
            return refs[2 * at + 1][...].astype(F32)
        both = refs[at][block_rows:, :].astype(F32)
        return jnp.concatenate([both[:capacity], both[capacity:]], axis=1)

    def lower(gain_ref, mask_ref, dq_ref, dv_ref, *refs):
        part_refs, out_ref, half_ref = refs[:-2], refs[-2], refs[-1]
        lane = lax.axis_index("lane")
        scaled = gain_ref[:, pl.ds(pl.multiple_of(lane * lane_width, lane_width), lane_width)]
        taken = jnp.concatenate(
            [slots_of(part_refs, step) for step in range(owners_count)], axis=0
        )
        taken = (taken * scaled).astype(BF16)
        contract = (((1,), (1,)), ((), ()))
        for at, ref in enumerate((dq_ref, dv_ref)):
            every = mask_ref[:, at * low_cols : (at + 1) * low_cols] * lax.dot_general(
                taken, ref[...], contract, preferred_element_type=F32
            )
            picked = every[:, :rank]
            for near in range(1, nearby):
                picked = picked + every[:, near * rank : (near + 1) * rank]
            out_ref[:, at * rank : (at + 1) * rank] = picked
        me = lax.axis_index("adapter")
        first = me * base_width + lax.rem(lane, 2) * half
        scaled = gain_ref[:, pl.ds(pl.multiple_of(first, half), half)]
        for step in range(owners_count):
            start = pl.multiple_of(jnp.bitwise_xor(me, step) * block_rows, block_rows)
            half_ref[pl.ds(start, block_rows), :] = (
                base_of(part_refs, step).astype(F32) * scaled
            ).astype(BF16)

    low, near_half = call(
        lower, "lower",
        [
            jax.ShapeDtypeStruct((slots, 2 * rank), F32),
            jax.ShapeDtypeStruct((rows, half), BF16),
        ],
        [VMEM] * (4 + len(arrived)), [VMEM] * 2,
        (gain, mask, w_query_down, w_value_down, *arrived),
        moved=MIB,
    )
    far_half = partner(near_half, "lane", 1)
    lows = [low] + [partner(low, "lane", step) for step in range(1, lane_count)]

    def project(near_ref, far_ref, wq_ref, wk_ref, wv_ref, out_ref, x_ref):
        side = lax.rem(lax.axis_index("lane"), 2)
        x_ref[:, pl.ds(pl.multiple_of(side * half, half), half)] = near_ref[...]
        x_ref[:, pl.ds(pl.multiple_of((1 - side) * half, half), half)] = far_ref[...]
        tile = min(1024, query_cols)
        for at in range(0, query_cols, tile):
            out_ref[:, at : at + tile] = jnp.dot(
                x_ref[...], wq_ref[:, at : at + tile], preferred_element_type=F32
            )
        out_ref[:, query_cols : query_cols + kv_cols] = jnp.dot(
            x_ref[...], wk_ref[...], preferred_element_type=F32
        )
        out_ref[:, query_cols + kv_cols :] = jnp.dot(
            x_ref[...], wv_ref[...], preferred_element_type=F32
        )

    based = call(
        project, "project", jax.ShapeDtypeStruct((rows, all_cols), F32),
        [VMEM] * 5, VMEM, (near_half, far_half, w_query, w_key, w_value),
        scratch=[pltpu.VMEM((rows, base_width), BF16)],
        flops=2 * rows * base_width * all_cols, moved=10 * MIB,
    )

    def raise_up(seen_ref, mask_ref, based_ref, uq_ref, uv_ref, *refs):
        low_refs, out_refs, sum_ref = refs[:lane_count], refs[lane_count:-1], refs[-1]
        me = lax.axis_index("adapter")
        total = low_refs[0][...]
        for ref in low_refs[1:]:
            total = total + ref[...]
        spread = [total[:, :rank]] * nearby + [total[:, rank:]] * nearby
        spread = jnp.concatenate(spread, axis=1) * mask_ref[...]
        lowered = lax.dot_general(
            seen_ref[...], spread.astype(BF16), (((0,), (0,)), ((), ())),
            preferred_element_type=F32,
        ).astype(BF16)
        for at in range(0, query_cols, 1024):
            stop = min(at + 1024, query_cols)
            sum_ref[:, at:stop] = based_ref[:, at:stop] + ADAPTER_SCALE * jnp.dot(
                lowered[:, :low_cols], uq_ref[:, at:stop], preferred_element_type=F32
            )
        middle = slice(query_cols, query_cols + kv_cols)
        last = slice(query_cols + kv_cols, all_cols)
        sum_ref[:, middle] = based_ref[:, middle]
        sum_ref[:, last] = based_ref[:, last] + ADAPTER_SCALE * jnp.dot(
            lowered[:, low_cols:], uv_ref[...], preferred_element_type=F32
        )
        for step in range(owners_count):
            start = pl.multiple_of(jnp.bitwise_xor(me, step) * block_rows, block_rows)
            out_refs[step][...] = sum_ref[pl.ds(start, block_rows), :].astype(out_refs[step].dtype)

    parts = call(
        raise_up, "raise_up",
        [
            jax.ShapeDtypeStruct((block_rows, all_cols), BF16 if step else F32)
            for step in range(owners_count)
        ],
        [VMEM] * (5 + lane_count), [VMEM] * owners_count,
        (seen, mask, based, query_up, value_up, *lows),
        scratch=[pltpu.VMEM((rows, all_cols), F32)],
    )
    parts = [
        partner(parts[step], "adapter", step) for step in reversed(range(1, owners_count))
    ] + [parts[0]]

    def finish(length_ref, scale_ref, k_ref, v_ref, *refs):
        part_refs = refs[:owners_count]
        out_ref, fresh_ref, sum_ref, q_ref, s_ref, o_ref = refs[owners_count:]
        summed = part_refs[-1][...]
        for ref in part_refs[:-1]:
            summed = summed + ref[...].astype(F32)
        summed = (summed * scale_ref[:, :1]).astype(BF16)
        key_new = summed[:, query_cols : query_cols + kv_cols]
        value_new = summed[:, query_cols + kv_cols :]
        fresh_ref[...] = jnp.stack([key_new, value_new], axis=1)
        sum_ref[...] = summed.astype(F32)
        for head in range(heads):
            q_ref[:, head, :] = sum_ref[:, head * head_dim : (head + 1) * head_dim]
        scale = head_dim ** (-0.5)
        twin = 2 * group_size
        spot = iota((twin, context), 1).astype(F32)
        top = iota((twin, 1), 0) < group_size
        keep = jnp.where(top, 1.0, 0.0)

        def pair_of(index):
            return divmod(index, kv_local), divmod(index + 1, kv_local)

        def stacked(index, start):
            (row_a, group_a), (row_b, group_b) = pair_of(index)
            at_a, at_b = start + group_a * head_dim, start + group_b * head_dim
            return jnp.where(
                top,
                sum_ref[row_a : row_a + 1, at_a : at_a + head_dim],
                sum_ref[row_b : row_b + 1, at_b : at_b + head_dim],
            )

        def asked_of(index):
            (row_a, group_a), (row_b, group_b) = pair_of(index)
            return jnp.concatenate(
                [
                    q_ref[row_a, group_a * group_size : (group_a + 1) * group_size, :],
                    q_ref[row_b, group_b * group_size : (group_b + 1) * group_size, :],
                ],
                axis=0,
            )

        def scores_of(index, asked):
            (row_a, group_a), (row_b, group_b) = pair_of(index)
            wide = jnp.concatenate([asked * keep, asked * (1.0 - keep)], axis=1).astype(BF16)
            both = jnp.concatenate([k_ref[row_a, group_a], k_ref[row_b, group_b]], axis=1)
            scores = lax.dot_general(
                wide, both, (((1,), (1,)), ((), ())), preferred_element_type=F32
            )
            length = jnp.where(
                top, length_ref[row_a : row_a + 1, :], length_ref[row_b : row_b + 1, :]
            )
            return jnp.where(spot < length, scores * scale, -jnp.inf)

        def mixed_of(index, weights):
            (row_a, group_a), (row_b, group_b) = pair_of(index)
            both = jnp.concatenate([v_ref[row_a, group_a], v_ref[row_b, group_b]], axis=1)
            mixed = jnp.dot(weights.astype(BF16), both, preferred_element_type=F32)
            return jnp.concatenate(
                [mixed[:group_size, :head_dim], mixed[group_size:, head_dim:]], axis=0
            )

        def put(index, mixed):
            (row_a, group_a), (row_b, group_b) = pair_of(index)
            o_ref[row_a, group_a * group_size : (group_a + 1) * group_size, :] = mixed[:group_size]
            o_ref[row_b, group_b * group_size : (group_b + 1) * group_size, :] = mixed[group_size:]

        pairs = range(0, block_rows * kv_local, 2)
        own = []
        for index in pairs:
            asked = asked_of(index)
            s_ref[index // 2] = scores_of(index, asked)
            own.append(jnp.sum(asked * stacked(index, query_cols), axis=1, keepdims=True))
        own_score = jnp.stack(own) * scale
        scores = s_ref[...]
        peak = jnp.maximum(jnp.max(scores, axis=2, keepdims=True), own_score)
        lifted = jnp.exp(scores - peak)
        own_lift = jnp.exp(own_score - peak)
        inverse = 1.0 / (jnp.sum(lifted, axis=2, keepdims=True) + own_lift)
        s_ref[...] = lifted * inverse
        own_weight = (own_lift * inverse).astype(BF16).astype(F32)
        for index in pairs:
            mixed = mixed_of(index, s_ref[index // 2])
            put(index, mixed + own_weight[index // 2] * stacked(index, query_cols + kv_cols))
        for head in range(heads):
            out_ref[:, head * head_dim : (head + 1) * head_dim] = o_ref[:, head, :].astype(BF16)

    attended, fresh = call(
        finish, "finish",
        [
            jax.ShapeDtypeStruct((block_rows, query_cols), BF16),
            jax.ShapeDtypeStruct((block_rows, 2, kv_cols), BF16),
        ],
        [VMEM] * (4 + owners_count), [VMEM] * 2,
        (row_length, row_scale, cached_key_rows, cached_value_rows, *parts),
        scratch=[
            pltpu.VMEM((block_rows, all_cols), F32),
            pltpu.VMEM((block_rows, heads, head_dim), F32),
            pltpu.VMEM((block_rows * kv_local // 2, 2 * group_size, context), F32),
            pltpu.VMEM((block_rows, heads, head_dim), F32),
        ],
    )
    return (attended, fresh)


def solution(mesh):
    in_specs = (
        P(("groups", "adapter"), None),
        P(),
        P("adapter", "lane"),
        P("adapter", "lane"),
        P("adapter", "lane"),
        P("adapter", "lane", None),
        P("adapter", None, "lane"),
        P("adapter", "lane", None),
        P("adapter", None, "lane"),
        P(("groups", "adapter"), "lane", None, None),
        P(("groups", "adapter"), "lane", None, None),
        P("groups"),
        P(("groups", "adapter")),
    )
    out_specs = (P(("groups", "adapter"), "lane"), P(("groups", "adapter"), None, "lane"))
    return jax.shard_map(
        on_device, mesh=mesh, in_specs=in_specs, out_specs=out_specs, check_vma=False
    )
```

```python
import jax
import jax.numpy as jnp
from jax import lax
from jax.experimental import pallas as pl
from jax.experimental.pallas import tpu as pltpu
from jax.sharding import PartitionSpec as P

EPS = 1e-05
ADAPTER_SCALE = 0.5
MIB = 2**20
F32 = jnp.float32
BF16 = jnp.bfloat16
VMEM = pl.BlockSpec(memory_space=pltpu.VMEM)
HBM = pl.BlockSpec(memory_space=pltpu.HBM)


def partner(array, axis, step):
    count = lax.axis_size(axis)
    return lax.ppermute(array, axis, [(i, i ^ step) for i in range(count)])


def call(body, name, outs, in_specs, out_specs, args, scratch=(), limit=16, flops=0, moved=0):
    return pl.pallas_call(
        body,
        name=name,
        out_shape=outs,
        in_specs=in_specs,
        out_specs=out_specs,
        scratch_shapes=scratch,
        compiler_params=pltpu.CompilerParams(vmem_limit_bytes=limit * MIB),
        cost_estimate=pl.CostEstimate(flops=flops, bytes_accessed=moved, transcendentals=0),
    )(*args)


def in_hbm(array):
    return pltpu.with_memory_space_constraint(array, pltpu.HBM)


def iota(shape, axis):
    return lax.broadcasted_iota(jnp.int32, shape, axis)


def slot_map(ids, owner, block, capacity, block_rows, nearby):
    slots, rows = owner.shape[0], ids.shape[1]
    first = owner * nearby
    spot = iota((slots, rows), 1)
    hit = (ids >= first) & (ids < first + nearby)
    hit = hit & (spot >= block * block_rows) & (spot < (block + 1) * block_rows)
    before = (iota((rows, rows), 0) < iota((rows, rows), 1)).astype(BF16)
    place = jnp.dot(
        jnp.where(hit, 1.0, 0.0).astype(BF16), before, preferred_element_type=F32
    )
    which = lax.rem(iota((slots, rows), 0), capacity).astype(F32)
    return jnp.where(hit & (place == which), 1.0, 0.0)


def on_device(
    residual_input,
    attention_norm_gain,
    query_weight,
    key_weight,
    value_weight,
    query_down_weight,
    query_up_weight,
    value_down_weight,
    value_up_weight,
    cached_key_rows,
    cached_value_rows,
    row_adapter_index,
    cached_length,
):
    owners_count = lax.axis_size("adapter")
    lane_count = lax.axis_size("lane")
    block_rows, width = residual_input.shape
    nearby, _, rank = query_down_weight.shape
    capacity = max(2, 2 * block_rows // owners_count)
    lane_width = width // lane_count
    base_width = width // owners_count
    query_cols = query_weight.shape[1]
    kv_cols = key_weight.shape[1]
    all_cols = query_cols + 2 * kv_cols
    slots = owners_count * capacity
    rows = owners_count * block_rows
    low_cols = nearby * rank
    half = base_width // 2
    joined = 2 * half == lane_width
    kv_local, context, head_dim = cached_key_rows.shape[1:]
    group_size = query_cols // head_dim // kv_local
    heads = kv_local * group_size

    ids = row_adapter_index.reshape(1, rows)
    gain = attention_norm_gain.reshape(1, width)
    query_down = jnp.swapaxes(query_down_weight, 1, 2).reshape(low_cols, lane_width)
    value_down = jnp.swapaxes(value_down_weight, 1, 2).reshape(low_cols, lane_width)
    query_up = query_up_weight.reshape(low_cols, query_cols)
    value_up = value_up_weight.reshape(low_cols, kv_cols)

    def prepare(ids_ref, x_ref, *refs):
        out_refs, chosen_ids, part, sems = refs[:-3], refs[-3], refs[-2], refs[-1]
        me = lax.axis_index("adapter")
        lane = lax.axis_index("lane")
        lane_at = pl.ds(pl.multiple_of(lane * lane_width, lane_width), lane_width)
        copies = [
            pltpu.make_async_copy(ids_ref, chosen_ids, sems.at[owners_count]),
            pltpu.make_async_copy(x_ref.at[:, lane_at], part, sems.at[owners_count + 1]),
        ]
        for step in range(owners_count):
            other = jnp.bitwise_xor(me, step)
            at = pl.ds(pl.multiple_of(other * base_width + lax.rem(lane, 2) * half, half), half)
            target = out_refs[step].at[:block_rows, :] if joined else out_refs[2 * step]
            copies.append(pltpu.make_async_copy(x_ref.at[:, at], target, sems.at[step]))
        for copy in copies:
            copy.start()
        copies[0].wait()
        owner = jnp.bitwise_xor(me, iota((slots, 1), 0) // capacity)
        chosen = slot_map(
            chosen_ids[...], owner, jnp.full((slots, 1), me), capacity, block_rows, nearby
        )
        fold = lax.rem(iota((rows, block_rows), 0), block_rows) == iota((rows, block_rows), 1)
        chosen = jnp.dot(
            chosen.astype(BF16), jnp.where(fold, 1.0, 0.0).astype(BF16), preferred_element_type=F32
        )
        copies[1].wait()
        placed = jnp.dot(chosen.astype(BF16), part[...], preferred_element_type=F32)
        for step in range(owners_count):
            mine = placed[step * capacity : (step + 1) * capacity]
            if joined:
                out_refs[step][block_rows:, :] = jnp.concatenate(
                    [mine[:, :half], mine[:, half:]], axis=0
                ).astype(BF16)
            else:
                out_refs[2 * step + 1][...] = mine.astype(BF16)
        for copy in copies[2:]:
            copy.wait()

    if joined:
        shapes = [jax.ShapeDtypeStruct((block_rows + 2 * capacity, half), BF16)] * owners_count
    else:
        shapes = [
            jax.ShapeDtypeStruct((block_rows, half), BF16),
            jax.ShapeDtypeStruct((capacity, lane_width), BF16),
        ] * owners_count
    sent = call(
        prepare, "prepare", shapes, [HBM] * 2, [VMEM] * len(shapes),
        (in_hbm(ids), in_hbm(residual_input)),
        scratch=[
            pltpu.VMEM((1, rows), jnp.int32),
            pltpu.VMEM((block_rows, lane_width), BF16),
            pltpu.SemaphoreType.DMA((owners_count + 2,)),
        ],
        moved=2**19,
    )
    per = len(sent) // owners_count
    first_order = list(reversed(range(1, owners_count)))
    arrived = [
        partner(piece, "adapter", step)
        for step in first_order
        for piece in sent[per * step : per * (step + 1)]
    ] + list(sent[:per])

    def place_of(step):
        return first_order.index(step) if step else owners_count - 1

    held = (query_down, value_down, query_weight, key_weight, value_weight)

    def survey(ids_ref, x_ref, length_ref, *refs):
        count = len(held)
        rms_ref, seen_ref, mask_ref, many_ref, ids_copy, x_copy, length_copy, sems = refs[2 * count :]
        copies = [
            pltpu.make_async_copy(ids_ref, ids_copy, sems.at[0]),
            pltpu.make_async_copy(x_ref, x_copy, sems.at[1]),
            pltpu.make_async_copy(length_ref, length_copy, sems.at[2]),
        ] + [
            pltpu.make_async_copy(refs[i], refs[count + i], sems.at[3 + i]) for i in range(count)
        ]
        for copy in copies:
            copy.start()
        copies[0].wait()
        me = lax.axis_index("adapter")
        block = jnp.bitwise_xor(me, iota((slots, 1), 0) // capacity)
        seen = slot_map(
            ids_copy[...], jnp.full((slots, 1), me), block, capacity, block_rows, nearby
        )
        seen_ref[...] = seen.astype(BF16)
        column = lax.rem(iota((slots, 2 * low_cols), 1) // rank, nearby)
        mask = jnp.zeros((slots, 2 * low_cols), F32)
        for near in range(nearby):
            uses = jnp.where(ids_copy[...] == me * nearby + near, seen, 0.0)
            uses = jnp.sum(uses, axis=1, keepdims=True)
            mask = jnp.where(column == near, uses, mask)
        mask_ref[...] = mask
        copies[2].wait()
        same = iota((block_rows, block_rows), 0) == iota((block_rows, block_rows), 1)
        many = jnp.sum(
            jnp.where(same, length_copy[...].astype(F32), 0.0), axis=1, keepdims=True
        )
        many_ref[...] = jnp.broadcast_to(many, many_ref.shape)
        copies[1].wait()
        x = x_copy[...].astype(F32)
        mean = jnp.sum(x * x, axis=1, keepdims=True) * (1.0 / width)
        rms_ref[...] = jnp.broadcast_to(lax.rsqrt(mean + EPS), rms_ref.shape)
        for copy in copies[3:]:
            copy.wait()

    (w_query_down, w_value_down, w_query, w_key, w_value, row_scale, seen, mask,
     row_length) = call(
        survey, "survey",
        [pltpu.VMEM(a.shape, a.dtype) for a in held]
        + [
            jax.ShapeDtypeStruct((block_rows, 128), F32),
            jax.ShapeDtypeStruct((slots, rows), BF16),
            jax.ShapeDtypeStruct((slots, 2 * low_cols), F32),
            jax.ShapeDtypeStruct((block_rows, context), F32),
        ],
        [HBM] * (3 + len(held)), [VMEM] * (4 + len(held)),
        (in_hbm(ids), in_hbm(residual_input), in_hbm(cached_length.reshape(1, block_rows)),
         *(in_hbm(a) for a in held)),
        scratch=[
            pltpu.VMEM((1, rows), jnp.int32),
            pltpu.VMEM((block_rows, width), BF16),
            pltpu.VMEM((1, block_rows), jnp.int32),
            pltpu.SemaphoreType.DMA((3 + len(held),)),
        ],
        moved=12 * MIB,
    )

    def base_of(refs, step):
        at = place_of(step)
        return refs[at][:block_rows, :] if joined else refs[2 * at][...]

    def slots_of(refs, step):
        at = place_of(step)
        if not joined:
            return refs[2 * at + 1][...].astype(F32)
        both = refs[at][block_rows:, :].astype(F32)
        return jnp.concatenate([both[:capacity], both[capacity:]], axis=1)

    def lower(gain_ref, mask_ref, dq_ref, dv_ref, *refs):
        part_refs, out_ref, half_ref = refs[:-2], refs[-2], refs[-1]
        lane = lax.axis_index("lane")
        scaled = gain_ref[:, pl.ds(pl.multiple_of(lane * lane_width, lane_width), lane_width)]
        taken = jnp.concatenate(
            [slots_of(part_refs, step) for step in range(owners_count)], axis=0
        )
        taken = (taken * scaled).astype(BF16)
        contract = (((1,), (1,)), ((), ()))
        for at, ref in enumerate((dq_ref, dv_ref)):
            every = mask_ref[:, at * low_cols : (at + 1) * low_cols] * lax.dot_general(
                taken, ref[...], contract, preferred_element_type=F32
            )
            picked = every[:, :rank]
            for near in range(1, nearby):
                picked = picked + every[:, near * rank : (near + 1) * rank]
            out_ref[:, at * rank : (at + 1) * rank] = picked
        me = lax.axis_index("adapter")
        first = me * base_width + lax.rem(lane, 2) * half
        scaled = gain_ref[:, pl.ds(pl.multiple_of(first, half), half)]
        for step in range(owners_count):
            start = pl.multiple_of(jnp.bitwise_xor(me, step) * block_rows, block_rows)
            half_ref[pl.ds(start, block_rows), :] = (
                base_of(part_refs, step).astype(F32) * scaled
            ).astype(BF16)

    low, near_half = call(
        lower, "lower",
        [
            jax.ShapeDtypeStruct((slots, 2 * rank), F32),
            jax.ShapeDtypeStruct((rows, half), BF16),
        ],
        [VMEM] * (4 + len(arrived)), [VMEM] * 2,
        (gain, mask, w_query_down, w_value_down, *arrived),
        moved=MIB,
    )
    far_half = partner(near_half, "lane", 1)
    lows = [low] + [partner(low, "lane", step) for step in range(1, lane_count)]

    def project(near_ref, far_ref, wq_ref, wk_ref, wv_ref, out_ref, x_ref):
        side = lax.rem(lax.axis_index("lane"), 2)
        x_ref[:, pl.ds(pl.multiple_of(side * half, half), half)] = near_ref[...]
        x_ref[:, pl.ds(pl.multiple_of((1 - side) * half, half), half)] = far_ref[...]
        tile = min(1024, query_cols)
        for at in range(0, query_cols, tile):
            out_ref[:, at : at + tile] = jnp.dot(
                x_ref[...], wq_ref[:, at : at + tile], preferred_element_type=F32
            )
        out_ref[:, query_cols : query_cols + kv_cols] = jnp.dot(
            x_ref[...], wk_ref[...], preferred_element_type=F32
        )
        out_ref[:, query_cols + kv_cols :] = jnp.dot(
            x_ref[...], wv_ref[...], preferred_element_type=F32
        )

    based = call(
        project, "project", jax.ShapeDtypeStruct((rows, all_cols), F32),
        [VMEM] * 5, VMEM, (near_half, far_half, w_query, w_key, w_value),
        scratch=[pltpu.VMEM((rows, base_width), BF16)],
        flops=2 * rows * base_width * all_cols, moved=10 * MIB,
    )

    def raise_up(seen_ref, mask_ref, based_ref, uq_ref, uv_ref, *refs):
        low_refs, out_refs, sum_ref = refs[:lane_count], refs[lane_count:-1], refs[-1]
        me = lax.axis_index("adapter")
        total = low_refs[0][...]
        for ref in low_refs[1:]:
            total = total + ref[...]
        spread = [total[:, :rank]] * nearby + [total[:, rank:]] * nearby
        spread = jnp.concatenate(spread, axis=1) * mask_ref[...]
        lowered = lax.dot_general(
            seen_ref[...], spread.astype(BF16), (((0,), (0,)), ((), ())),
            preferred_element_type=F32,
        ).astype(BF16)
        for at in range(0, query_cols, 1024):
            stop = min(at + 1024, query_cols)
            sum_ref[:, at:stop] = based_ref[:, at:stop] + ADAPTER_SCALE * jnp.dot(
                lowered[:, :low_cols], uq_ref[:, at:stop], preferred_element_type=F32
            )
        middle = slice(query_cols, query_cols + kv_cols)
        last = slice(query_cols + kv_cols, all_cols)
        sum_ref[:, middle] = based_ref[:, middle]
        sum_ref[:, last] = based_ref[:, last] + ADAPTER_SCALE * jnp.dot(
            lowered[:, low_cols:], uv_ref[...], preferred_element_type=F32
        )
        for step in range(owners_count):
            start = pl.multiple_of(jnp.bitwise_xor(me, step) * block_rows, block_rows)
            out_refs[step][...] = sum_ref[pl.ds(start, block_rows), :].astype(out_refs[step].dtype)

    parts = call(
        raise_up, "raise_up",
        [
            jax.ShapeDtypeStruct((block_rows, all_cols), BF16 if step else F32)
            for step in range(owners_count)
        ],
        [VMEM] * (5 + lane_count), [VMEM] * owners_count,
        (seen, mask, based, query_up, value_up, *lows),
        scratch=[pltpu.VMEM((rows, all_cols), F32)],
    )
    parts = [
        partner(parts[step], "adapter", step) for step in [*range(2, owners_count), 1]
    ] + [parts[0]]

    def finish(length_ref, scale_ref, k_ref, v_ref, *refs):
        part_refs = refs[:owners_count]
        out_ref, fresh_ref, sum_ref, q_ref, s_ref, o_ref = refs[owners_count:]
        summed = part_refs[-1][...]
        for ref in part_refs[:-1]:
            summed = summed + ref[...].astype(F32)
        summed = (summed * scale_ref[:, :1]).astype(BF16)
        key_new = summed[:, query_cols : query_cols + kv_cols]
        value_new = summed[:, query_cols + kv_cols :]
        fresh_ref[...] = jnp.stack([key_new, value_new], axis=1)
        sum_ref[...] = summed.astype(F32)
        for head in range(heads):
            q_ref[:, head, :] = sum_ref[:, head * head_dim : (head + 1) * head_dim]
        scale = head_dim ** (-0.5)
        twin = 2 * group_size
        spot = iota((twin, context), 1).astype(F32)
        top = iota((twin, 1), 0) < group_size
        keep = jnp.where(top, 1.0, 0.0)

        def pair_of(index):
            return divmod(index, kv_local), divmod(index + 1, kv_local)

        def stacked(index, start):
            (row_a, group_a), (row_b, group_b) = pair_of(index)
            at_a, at_b = start + group_a * head_dim, start + group_b * head_dim
            return jnp.where(
                top,
                sum_ref[row_a : row_a + 1, at_a : at_a + head_dim],
                sum_ref[row_b : row_b + 1, at_b : at_b + head_dim],
            )

        def asked_of(index):
            (row_a, group_a), (row_b, group_b) = pair_of(index)
            return jnp.concatenate(
                [
                    q_ref[row_a, group_a * group_size : (group_a + 1) * group_size, :],
                    q_ref[row_b, group_b * group_size : (group_b + 1) * group_size, :],
                ],
                axis=0,
            )

        def scores_of(index, asked):
            (row_a, group_a), (row_b, group_b) = pair_of(index)
            wide = jnp.concatenate([asked * keep, asked * (1.0 - keep)], axis=1).astype(BF16)
            both = jnp.concatenate([k_ref[row_a, group_a], k_ref[row_b, group_b]], axis=1)
            scores = lax.dot_general(
                wide, both, (((1,), (1,)), ((), ())), preferred_element_type=F32
            )
            length = jnp.where(
                top, length_ref[row_a : row_a + 1, :], length_ref[row_b : row_b + 1, :]
            )
            return jnp.where(spot < length, scores * scale, -jnp.inf)

        def mixed_of(index, weights):
            (row_a, group_a), (row_b, group_b) = pair_of(index)
            both = jnp.concatenate([v_ref[row_a, group_a], v_ref[row_b, group_b]], axis=1)
            mixed = jnp.dot(weights.astype(BF16), both, preferred_element_type=F32)
            return jnp.concatenate(
                [mixed[:group_size, :head_dim], mixed[group_size:, head_dim:]], axis=0
            )

        def put(index, mixed):
            (row_a, group_a), (row_b, group_b) = pair_of(index)
            o_ref[row_a, group_a * group_size : (group_a + 1) * group_size, :] = mixed[:group_size]
            o_ref[row_b, group_b * group_size : (group_b + 1) * group_size, :] = mixed[group_size:]

        pairs = range(0, block_rows * kv_local, 2)
        own = []
        for index in pairs:
            asked = asked_of(index)
            s_ref[index // 2] = scores_of(index, asked)
            own.append(jnp.sum(asked * stacked(index, query_cols), axis=1, keepdims=True))
        own_score = jnp.stack(own) * scale
        scores = s_ref[...]
        peak = jnp.maximum(jnp.max(scores, axis=2, keepdims=True), own_score)
        lifted = jnp.exp(scores - peak)
        own_lift = jnp.exp(own_score - peak)
        inverse = 1.0 / (jnp.sum(lifted, axis=2, keepdims=True) + own_lift)
        s_ref[...] = lifted * inverse
        own_weight = (own_lift * inverse).astype(BF16).astype(F32)
        for index in pairs:
            mixed = mixed_of(index, s_ref[index // 2])
            put(index, mixed + own_weight[index // 2] * stacked(index, query_cols + kv_cols))
        for head in range(heads):
            out_ref[:, head * head_dim : (head + 1) * head_dim] = o_ref[:, head, :].astype(BF16)

    attended, fresh = call(
        finish, "finish",
        [
            jax.ShapeDtypeStruct((block_rows, query_cols), BF16),
            jax.ShapeDtypeStruct((block_rows, 2, kv_cols), BF16),
        ],
        [VMEM] * (4 + owners_count), [VMEM] * 2,
        (row_length, row_scale, cached_key_rows, cached_value_rows, *parts),
        scratch=[
            pltpu.VMEM((block_rows, all_cols), F32),
            pltpu.VMEM((block_rows, heads, head_dim), F32),
            pltpu.VMEM((block_rows * kv_local // 2, 2 * group_size, context), F32),
            pltpu.VMEM((block_rows, heads, head_dim), F32),
        ],
    )
    return (attended, fresh)


def solution(mesh):
    in_specs = (
        P(("groups", "adapter"), None),
        P(),
        P("adapter", "lane"),
        P("adapter", "lane"),
        P("adapter", "lane"),
        P("adapter", "lane", None),
        P("adapter", None, "lane"),
        P("adapter", "lane", None),
        P("adapter", None, "lane"),
        P(("groups", "adapter"), "lane", None, None),
        P(("groups", "adapter"), "lane", None, None),
        P("groups"),
        P(("groups", "adapter")),
    )
    out_specs = (P(("groups", "adapter"), "lane"), P(("groups", "adapter"), None, "lane"))
    return jax.shard_map(
        on_device, mesh=mesh, in_specs=in_specs, out_specs=out_specs, check_vma=False
    )
```

```python
import jax
import jax.numpy as jnp
from jax import lax
from jax.experimental import pallas as pl
from jax.experimental.pallas import tpu as pltpu
from jax.sharding import PartitionSpec as P

EPS = 1e-05
ADAPTER_SCALE = 0.5
MIB = 2**20
F32 = jnp.float32
BF16 = jnp.bfloat16
VMEM = pl.BlockSpec(memory_space=pltpu.VMEM)
HBM = pl.BlockSpec(memory_space=pltpu.HBM)


def partner(array, axis, step):
    count = lax.axis_size(axis)
    return lax.ppermute(array, axis, [(i, i ^ step) for i in range(count)])


def call(body, name, outs, in_specs, out_specs, args, scratch=(), limit=16, flops=0, moved=0):
    return pl.pallas_call(
        body,
        name=name,
        out_shape=outs,
        in_specs=in_specs,
        out_specs=out_specs,
        scratch_shapes=scratch,
        compiler_params=pltpu.CompilerParams(vmem_limit_bytes=limit * MIB),
        cost_estimate=pl.CostEstimate(flops=flops, bytes_accessed=moved, transcendentals=0),
    )(*args)


def in_hbm(array):
    return pltpu.with_memory_space_constraint(array, pltpu.HBM)


def iota(shape, axis):
    return lax.broadcasted_iota(jnp.int32, shape, axis)


def slot_map(ids, owner, block, capacity, block_rows, nearby):
    slots, rows = owner.shape[0], ids.shape[1]
    first = owner * nearby
    spot = iota((slots, rows), 1)
    hit = (ids >= first) & (ids < first + nearby)
    hit = hit & (spot >= block * block_rows) & (spot < (block + 1) * block_rows)
    before = (iota((rows, rows), 0) < iota((rows, rows), 1)).astype(BF16)
    place = jnp.dot(
        jnp.where(hit, 1.0, 0.0).astype(BF16), before, preferred_element_type=F32
    )
    which = lax.rem(iota((slots, rows), 0), capacity).astype(F32)
    return jnp.where(hit & (place == which), 1.0, 0.0)


def on_device(
    residual_input,
    attention_norm_gain,
    query_weight,
    key_weight,
    value_weight,
    query_down_weight,
    query_up_weight,
    value_down_weight,
    value_up_weight,
    cached_key_rows,
    cached_value_rows,
    row_adapter_index,
    cached_length,
):
    owners_count = lax.axis_size("adapter")
    lane_count = lax.axis_size("lane")
    block_rows, width = residual_input.shape
    nearby, _, rank = query_down_weight.shape
    capacity = max(2, 2 * block_rows // owners_count)
    lane_width = width // lane_count
    base_width = width // owners_count
    query_cols = query_weight.shape[1]
    kv_cols = key_weight.shape[1]
    all_cols = query_cols + 2 * kv_cols
    slots = owners_count * capacity
    rows = owners_count * block_rows
    low_cols = nearby * rank
    half = base_width // 2
    joined = 2 * half == lane_width
    kv_local, context, head_dim = cached_key_rows.shape[1:]
    group_size = query_cols // head_dim // kv_local
    heads = kv_local * group_size

    ids = row_adapter_index.reshape(1, rows)
    gain = attention_norm_gain.reshape(1, width)
    query_down = jnp.swapaxes(query_down_weight, 1, 2).reshape(low_cols, lane_width)
    value_down = jnp.swapaxes(value_down_weight, 1, 2).reshape(low_cols, lane_width)
    query_up = query_up_weight.reshape(low_cols, query_cols)
    value_up = value_up_weight.reshape(low_cols, kv_cols)

    def prepare(ids_ref, x_ref, *refs):
        out_refs, chosen_ids, part, sems = refs[:-3], refs[-3], refs[-2], refs[-1]
        me = lax.axis_index("adapter")
        lane = lax.axis_index("lane")
        lane_at = pl.ds(pl.multiple_of(lane * lane_width, lane_width), lane_width)
        copies = [
            pltpu.make_async_copy(ids_ref, chosen_ids, sems.at[owners_count]),
            pltpu.make_async_copy(x_ref.at[:, lane_at], part, sems.at[owners_count + 1]),
        ]
        for step in range(owners_count):
            other = jnp.bitwise_xor(me, step)
            at = pl.ds(pl.multiple_of(other * base_width + lax.rem(lane, 2) * half, half), half)
            target = out_refs[step].at[:block_rows, :] if joined else out_refs[2 * step]
            copies.append(pltpu.make_async_copy(x_ref.at[:, at], target, sems.at[step]))
        for copy in copies:
            copy.start()
        owner = jnp.bitwise_xor(me, iota((slots, rows), 0) // capacity) * nearby
        row, spot = iota((rows, block_rows), 0), iota((rows, block_rows), 1) + me * block_rows
        fold = jnp.where(row == spot, 1.0, 0.0).astype(BF16)
        before = jnp.where((row < spot) & (row >= me * block_rows), 1.0, 0.0).astype(BF16)
        which = lax.rem(iota((slots, block_rows), 0), capacity).astype(F32)
        copies[0].wait()
        taken = chosen_ids[...]
        hit = jnp.where((taken >= owner) & (taken < owner + nearby), 1.0, 0.0).astype(BF16)
        mine = jnp.dot(hit, fold, preferred_element_type=F32)
        place = jnp.dot(hit, before, preferred_element_type=F32)
        chosen = jnp.where((mine > 0.5) & (place == which), 1.0, 0.0)
        copies[1].wait()
        placed = jnp.dot(chosen.astype(BF16), part[...], preferred_element_type=F32)
        for step in range(owners_count):
            mine = placed[step * capacity : (step + 1) * capacity]
            if joined:
                out_refs[step][block_rows:, :] = jnp.concatenate(
                    [mine[:, :half], mine[:, half:]], axis=0
                ).astype(BF16)
            else:
                out_refs[2 * step + 1][...] = mine.astype(BF16)
        for copy in copies[2:]:
            copy.wait()

    if joined:
        shapes = [jax.ShapeDtypeStruct((block_rows + 2 * capacity, half), BF16)] * owners_count
    else:
        shapes = [
            jax.ShapeDtypeStruct((block_rows, half), BF16),
            jax.ShapeDtypeStruct((capacity, lane_width), BF16),
        ] * owners_count
    sent = call(
        prepare, "prepare", shapes, [HBM] * 2, [VMEM] * len(shapes),
        (in_hbm(ids), in_hbm(residual_input)),
        scratch=[
            pltpu.VMEM((1, rows), jnp.int32),
            pltpu.VMEM((block_rows, lane_width), BF16),
            pltpu.SemaphoreType.DMA((owners_count + 2,)),
        ],
        moved=2**19,
    )
    per = len(sent) // owners_count
    first_order = list(reversed(range(1, owners_count)))
    arrived = [
        partner(piece, "adapter", step)
        for step in first_order
        for piece in sent[per * step : per * (step + 1)]
    ] + list(sent[:per])

    def place_of(step):
        return first_order.index(step) if step else owners_count - 1

    held = (query_down, value_down, query_weight, key_weight, value_weight)
    made = [
        pltpu.VMEM((2 * low_cols, lane_width), BF16),
        *(pltpu.VMEM(a.shape, a.dtype) for a in held[2:]),
    ]

    def survey(ids_ref, x_ref, length_ref, *refs):
        count = len(held)
        rms_ref, seen_ref, mask_ref, many_ref, ids_copy, x_copy, length_copy, sems = refs[2 * count - 1 :]
        targets = [
            refs[count].at[:low_cols, :], refs[count].at[low_cols:, :],
            *refs[count + 1 : 2 * count - 1],
        ]
        copies = [
            pltpu.make_async_copy(ids_ref, ids_copy, sems.at[0]),
            pltpu.make_async_copy(x_ref, x_copy, sems.at[1]),
            pltpu.make_async_copy(length_ref, length_copy, sems.at[2]),
        ] + [
            pltpu.make_async_copy(refs[i], targets[i], sems.at[3 + i]) for i in range(count)
        ]
        for copy in copies:
            copy.start()
        copies[0].wait()
        me = lax.axis_index("adapter")
        block = jnp.bitwise_xor(me, iota((slots, 1), 0) // capacity)
        seen = slot_map(
            ids_copy[...], jnp.full((slots, 1), me), block, capacity, block_rows, nearby
        )
        spot = iota((rows, rows), 1)
        mirror = jnp.bitwise_xor(me, spot // block_rows) * block_rows + lax.rem(spot, block_rows)
        mirror = jnp.where(iota((rows, rows), 0) == mirror, 1.0, 0.0).astype(BF16)
        seen_ref[...] = jnp.dot(
            seen.astype(BF16), mirror, preferred_element_type=F32
        ).astype(BF16)
        column = lax.rem(iota((slots, 2 * low_cols), 1) // rank, nearby)
        mask = jnp.zeros((slots, 2 * low_cols), F32)
        for near in range(nearby):
            uses = jnp.where(ids_copy[...] == me * nearby + near, seen, 0.0)
            uses = jnp.sum(uses, axis=1, keepdims=True)
            mask = jnp.where(column == near, uses, mask)
        mask_ref[...] = mask
        copies[2].wait()
        same = iota((block_rows, block_rows), 0) == iota((block_rows, block_rows), 1)
        many = jnp.sum(
            jnp.where(same, length_copy[...].astype(F32), 0.0), axis=1, keepdims=True
        )
        many_ref[...] = jnp.broadcast_to(many, many_ref.shape)
        copies[1].wait()
        x = x_copy[...].astype(F32)
        mean = jnp.sum(x * x, axis=1, keepdims=True) * (1.0 / width)
        rms_ref[...] = jnp.broadcast_to(lax.rsqrt(mean + EPS), rms_ref.shape)
        for copy in copies[3:]:
            copy.wait()

    (w_down, w_query, w_key, w_value, row_scale, seen, mask,
     row_length) = call(
        survey, "survey",
        made
        + [
            jax.ShapeDtypeStruct((block_rows, 128), F32),
            jax.ShapeDtypeStruct((slots, rows), BF16),
            jax.ShapeDtypeStruct((slots, 2 * low_cols), F32),
            jax.ShapeDtypeStruct((block_rows, context), F32),
        ],
        [HBM] * (3 + len(held)), [VMEM] * (4 + len(made)),
        (in_hbm(ids), in_hbm(residual_input), in_hbm(cached_length.reshape(1, block_rows)),
         *(in_hbm(a) for a in held)),
        scratch=[
            pltpu.VMEM((1, rows), jnp.int32),
            pltpu.VMEM((block_rows, width), BF16),
            pltpu.VMEM((1, block_rows), jnp.int32),
            pltpu.SemaphoreType.DMA((3 + len(held),)),
        ],
        moved=12 * MIB,
    )

    def base_of(refs, step):
        at = place_of(step)
        return refs[at][:block_rows, :] if joined else refs[2 * at][...]

    def slots_of(refs, step):
        at = place_of(step)
        if not joined:
            return refs[2 * at + 1][...].astype(F32)
        both = refs[at][block_rows:, :].astype(F32)
        return jnp.concatenate([both[:capacity], both[capacity:]], axis=1)

    def lower(gain_ref, mask_ref, down_ref, *refs):
        part_refs, out_ref, half_ref = refs[:-2], refs[-2], refs[-1]
        lane = lax.axis_index("lane")
        scaled = gain_ref[:, pl.ds(pl.multiple_of(lane * lane_width, lane_width), lane_width)]
        taken = jnp.concatenate(
            [slots_of(part_refs, step) for step in range(owners_count)], axis=0
        )
        taken = (taken * scaled).astype(BF16)
        contract = (((1,), (1,)), ((), ()))
        every = mask_ref[...] * lax.dot_general(
            taken, down_ref[...], contract, preferred_element_type=F32
        )
        for at in range(2):
            first = at * low_cols
            picked = every[:, first : first + rank]
            for near in range(1, nearby):
                picked = picked + every[:, first + near * rank : first + (near + 1) * rank]
            out_ref[:, at * rank : (at + 1) * rank] = picked
        me = lax.axis_index("adapter")
        first = me * base_width + lax.rem(lane, 2) * half
        scaled = gain_ref[:, pl.ds(pl.multiple_of(first, half), half)]
        for step in range(owners_count):
            half_ref[step * block_rows : (step + 1) * block_rows, :] = (
                base_of(part_refs, step).astype(F32) * scaled
            ).astype(BF16)

    low, near_half = call(
        lower, "lower",
        [
            jax.ShapeDtypeStruct((slots, 2 * rank), F32),
            jax.ShapeDtypeStruct((rows, half), BF16),
        ],
        [VMEM] * (3 + len(arrived)), [VMEM] * 2,
        (gain, mask, w_down, *arrived),
        moved=MIB,
    )
    far_half = partner(near_half, "lane", 1)
    lows = [low] + [partner(low, "lane", step) for step in range(1, lane_count)]

    def project(near_ref, far_ref, wq_ref, wk_ref, wv_ref, out_ref, x_ref):
        side = lax.rem(lax.axis_index("lane"), 2)
        x_ref[:, pl.ds(pl.multiple_of(side * half, half), half)] = near_ref[...]
        x_ref[:, pl.ds(pl.multiple_of((1 - side) * half, half), half)] = far_ref[...]
        tile = min(1024, query_cols)
        for at in range(0, query_cols, tile):
            out_ref[:, at : at + tile] = jnp.dot(
                x_ref[...], wq_ref[:, at : at + tile], preferred_element_type=F32
            )
        out_ref[:, query_cols : query_cols + kv_cols] = jnp.dot(
            x_ref[...], wk_ref[...], preferred_element_type=F32
        )
        out_ref[:, query_cols + kv_cols :] = jnp.dot(
            x_ref[...], wv_ref[...], preferred_element_type=F32
        )

    based = call(
        project, "project", jax.ShapeDtypeStruct((rows, all_cols), F32),
        [VMEM] * 5, VMEM, (near_half, far_half, w_query, w_key, w_value),
        scratch=[pltpu.VMEM((rows, base_width), BF16)],
        flops=2 * rows * base_width * all_cols, moved=10 * MIB,
    )

    def raise_up(seen_ref, mask_ref, based_ref, uq_ref, uv_ref, *refs):
        low_refs, out_refs = refs[:lane_count], refs[lane_count:]
        total = low_refs[0][...]
        for ref in low_refs[1:]:
            total = total + ref[...]
        spread = [total[:, :rank]] * nearby + [total[:, rank:]] * nearby
        spread = jnp.concatenate(spread, axis=1) * mask_ref[...]
        lowered = lax.dot_general(
            seen_ref[...], spread.astype(BF16), (((0,), (0,)), ((), ())),
            preferred_element_type=F32,
        ).astype(BF16)
        middle = slice(query_cols, query_cols + kv_cols)
        last = slice(query_cols + kv_cols, all_cols)
        tile = min(1024, query_cols)
        pieces = [(slice(at, at + tile), 0, uq_ref, at) for at in range(0, query_cols, tile)]
        pieces.append((last, low_cols, uv_ref, 0))
        for columns, first, weight_ref, at in pieces:
            size = columns.stop - columns.start
            raised = based_ref[:, columns] + ADAPTER_SCALE * jnp.dot(
                lowered[:, first : first + low_cols], weight_ref[:, at : at + size],
                preferred_element_type=F32,
            )
            for step in range(owners_count):
                out_refs[step][:, columns] = raised[
                    step * block_rows : (step + 1) * block_rows
                ].astype(out_refs[step].dtype)
        for step in range(owners_count):
            out_refs[step][:, middle] = based_ref[
                step * block_rows : (step + 1) * block_rows, middle
            ].astype(out_refs[step].dtype)

    parts = call(
        raise_up, "raise_up",
        [
            jax.ShapeDtypeStruct((block_rows, all_cols), BF16 if step else F32)
            for step in range(owners_count)
        ],
        [VMEM] * (5 + lane_count), [VMEM] * owners_count,
        (seen, mask, based, query_up, value_up, *lows),
    )
    parts = [
        partner(parts[step], "adapter", step) for step in [*range(2, owners_count), 1]
    ] + [parts[0]]

    def finish(length_ref, scale_ref, k_ref, v_ref, *refs):
        part_refs = refs[:owners_count]
        out_ref, fresh_ref, sum_ref, q_ref, s_ref, o_ref = refs[owners_count:]
        summed = part_refs[-1][...]
        for ref in part_refs[:-1]:
            summed = summed + ref[...].astype(F32)
        summed = (summed * scale_ref[:, :1]).astype(BF16)
        key_new = summed[:, query_cols : query_cols + kv_cols]
        value_new = summed[:, query_cols + kv_cols :]
        fresh_ref[...] = jnp.stack([key_new, value_new], axis=1)
        sum_ref[...] = summed.astype(F32)
        for head in range(heads):
            q_ref[:, head, :] = sum_ref[:, head * head_dim : (head + 1) * head_dim]
        scale = head_dim ** (-0.5)
        twin = 2 * group_size
        spot = iota((twin, context), 1).astype(F32)
        top = iota((twin, 1), 0) < group_size
        keep = jnp.where(top, 1.0, 0.0)

        def pair_of(index):
            return divmod(index, kv_local), divmod(index + 1, kv_local)

        def stacked(index, start):
            (row_a, group_a), (row_b, group_b) = pair_of(index)
            at_a, at_b = start + group_a * head_dim, start + group_b * head_dim
            return jnp.where(
                top,
                sum_ref[row_a : row_a + 1, at_a : at_a + head_dim],
                sum_ref[row_b : row_b + 1, at_b : at_b + head_dim],
            )

        def asked_of(index):
            (row_a, group_a), (row_b, group_b) = pair_of(index)
            return jnp.concatenate(
                [
                    q_ref[row_a, group_a * group_size : (group_a + 1) * group_size, :],
                    q_ref[row_b, group_b * group_size : (group_b + 1) * group_size, :],
                ],
                axis=0,
            )

        def scores_of(index, asked):
            (row_a, group_a), (row_b, group_b) = pair_of(index)
            wide = jnp.concatenate([asked * keep, asked * (1.0 - keep)], axis=1).astype(BF16)
            both = jnp.concatenate([k_ref[row_a, group_a], k_ref[row_b, group_b]], axis=1)
            scores = lax.dot_general(
                wide, both, (((1,), (1,)), ((), ())), preferred_element_type=F32
            )
            length = jnp.where(
                top, length_ref[row_a : row_a + 1, :], length_ref[row_b : row_b + 1, :]
            )
            return jnp.where(spot < length, scores * scale, -jnp.inf)

        def mixed_of(index, weights):
            (row_a, group_a), (row_b, group_b) = pair_of(index)
            both = jnp.concatenate([v_ref[row_a, group_a], v_ref[row_b, group_b]], axis=1)
            mixed = jnp.dot(weights.astype(BF16), both, preferred_element_type=F32)
            return jnp.concatenate(
                [mixed[:group_size, :head_dim], mixed[group_size:, head_dim:]], axis=0
            )

        def put(index, mixed):
            (row_a, group_a), (row_b, group_b) = pair_of(index)
            o_ref[row_a, group_a * group_size : (group_a + 1) * group_size, :] = mixed[:group_size]
            o_ref[row_b, group_b * group_size : (group_b + 1) * group_size, :] = mixed[group_size:]

        pairs = range(0, block_rows * kv_local, 2)
        own = []
        for index in pairs:
            asked = asked_of(index)
            s_ref[index // 2] = scores_of(index, asked)
            own.append(jnp.sum(asked * stacked(index, query_cols), axis=1, keepdims=True))
        own_score = jnp.stack(own) * scale
        scores = s_ref[...]
        peak = jnp.maximum(jnp.max(scores, axis=2, keepdims=True), own_score)
        lifted = jnp.exp(scores - peak)
        own_lift = jnp.exp(own_score - peak)
        inverse = 1.0 / (jnp.sum(lifted, axis=2, keepdims=True) + own_lift)
        s_ref[...] = lifted * inverse
        own_weight = (own_lift * inverse).astype(BF16).astype(F32)
        for index in pairs:
            mixed = mixed_of(index, s_ref[index // 2])
            put(index, mixed + own_weight[index // 2] * stacked(index, query_cols + kv_cols))
        for head in range(heads):
            out_ref[:, head * head_dim : (head + 1) * head_dim] = o_ref[:, head, :].astype(BF16)

    attended, fresh = call(
        finish, "finish",
        [
            jax.ShapeDtypeStruct((block_rows, query_cols), BF16),
            jax.ShapeDtypeStruct((block_rows, 2, kv_cols), BF16),
        ],
        [VMEM] * (4 + owners_count), [VMEM] * 2,
        (row_length, row_scale, cached_key_rows, cached_value_rows, *parts),
        scratch=[
            pltpu.VMEM((block_rows, all_cols), F32),
            pltpu.VMEM((block_rows, heads, head_dim), F32),
            pltpu.VMEM((block_rows * kv_local // 2, 2 * group_size, context), F32),
            pltpu.VMEM((block_rows, heads, head_dim), F32),
        ],
    )
    return (attended, fresh)


def solution(mesh):
    in_specs = (
        P(("groups", "adapter"), None),
        P(),
        P("adapter", "lane"),
        P("adapter", "lane"),
        P("adapter", "lane"),
        P("adapter", "lane", None),
        P("adapter", None, "lane"),
        P("adapter", "lane", None),
        P("adapter", None, "lane"),
        P(("groups", "adapter"), "lane", None, None),
        P(("groups", "adapter"), "lane", None, None),
        P("groups"),
        P(("groups", "adapter")),
    )
    out_specs = (P(("groups", "adapter"), "lane"), P(("groups", "adapter"), None, "lane"))
    return jax.shard_map(
        on_device, mesh=mesh, in_specs=in_specs, out_specs=out_specs, check_vma=False
    )
```

```python
import jax
import jax.numpy as jnp
from jax import lax
from jax.experimental import pallas as pl
from jax.experimental.pallas import tpu as pltpu
from jax.sharding import PartitionSpec as P

EPS = 1e-05
ADAPTER_SCALE = 0.5
MIB = 2**20
F32 = jnp.float32
BF16 = jnp.bfloat16
VMEM = pl.BlockSpec(memory_space=pltpu.VMEM)
HBM = pl.BlockSpec(memory_space=pltpu.HBM)


def partner(array, axis, step):
    count = lax.axis_size(axis)
    return lax.ppermute(array, axis, [(i, i ^ step) for i in range(count)])


def call(body, name, outs, in_specs, out_specs, args, scratch=(), limit=16, flops=0, moved=0):
    return pl.pallas_call(
        body,
        name=name,
        out_shape=outs,
        in_specs=in_specs,
        out_specs=out_specs,
        scratch_shapes=scratch,
        compiler_params=pltpu.CompilerParams(vmem_limit_bytes=limit * MIB),
        cost_estimate=pl.CostEstimate(flops=flops, bytes_accessed=moved, transcendentals=0),
    )(*args)


def in_hbm(array):
    return pltpu.with_memory_space_constraint(array, pltpu.HBM)


def iota(shape, axis):
    return lax.broadcasted_iota(jnp.int32, shape, axis)


def slot_map(ids, owner, block, capacity, block_rows, nearby):
    slots, rows = owner.shape[0], ids.shape[1]
    first = owner * nearby
    spot = iota((slots, rows), 1)
    hit = (ids >= first) & (ids < first + nearby)
    hit = hit & (spot >= block * block_rows) & (spot < (block + 1) * block_rows)
    before = (iota((rows, rows), 0) < iota((rows, rows), 1)).astype(BF16)
    place = jnp.dot(
        jnp.where(hit, 1.0, 0.0).astype(BF16), before, preferred_element_type=F32
    )
    which = lax.rem(iota((slots, rows), 0), capacity).astype(F32)
    return jnp.where(hit & (place == which), 1.0, 0.0)


def on_device(
    residual_input,
    attention_norm_gain,
    query_weight,
    key_weight,
    value_weight,
    query_down_weight,
    query_up_weight,
    value_down_weight,
    value_up_weight,
    cached_key_rows,
    cached_value_rows,
    row_adapter_index,
    cached_length,
):
    owners_count = lax.axis_size("adapter")
    lane_count = lax.axis_size("lane")
    block_rows, width = residual_input.shape
    nearby, _, rank = query_down_weight.shape
    capacity = max(2, 2 * block_rows // owners_count)
    lane_width = width // lane_count
    base_width = width // owners_count
    query_cols = query_weight.shape[1]
    kv_cols = key_weight.shape[1]
    all_cols = query_cols + 2 * kv_cols
    slots = owners_count * capacity
    rows = owners_count * block_rows
    low_cols = nearby * rank
    half = base_width // 2
    joined = 2 * half == lane_width
    kv_local, context, head_dim = cached_key_rows.shape[1:]
    group_size = query_cols // head_dim // kv_local
    heads = kv_local * group_size

    ids = row_adapter_index.reshape(1, rows)
    gain = attention_norm_gain.reshape(1, width)
    query_down = jnp.swapaxes(query_down_weight, 1, 2).reshape(low_cols, lane_width)
    value_down = jnp.swapaxes(value_down_weight, 1, 2).reshape(low_cols, lane_width)
    query_up = query_up_weight.reshape(low_cols, query_cols)
    value_up = value_up_weight.reshape(low_cols, kv_cols)

    def prepare(ids_ref, x_ref, *refs):
        out_refs, chosen_ids, part, sems = refs[:-3], refs[-3], refs[-2], refs[-1]
        me = lax.axis_index("adapter")
        lane = lax.axis_index("lane")
        lane_at = pl.ds(pl.multiple_of(lane * lane_width, lane_width), lane_width)
        copies = [
            pltpu.make_async_copy(ids_ref, chosen_ids, sems.at[owners_count]),
            pltpu.make_async_copy(x_ref.at[:, lane_at], part, sems.at[owners_count + 1]),
        ]
        for step in range(owners_count):
            other = jnp.bitwise_xor(me, step)
            at = pl.ds(pl.multiple_of(other * base_width + lax.rem(lane, 2) * half, half), half)
            target = out_refs[step].at[:block_rows, :] if joined else out_refs[2 * step]
            copies.append(pltpu.make_async_copy(x_ref.at[:, at], target, sems.at[step]))
        for copy in copies:
            copy.start()
        owner = jnp.bitwise_xor(me, iota((slots, rows), 0) // capacity) * nearby
        row, spot = iota((rows, block_rows), 0), iota((rows, block_rows), 1) + me * block_rows
        fold = jnp.where(row == spot, 1.0, 0.0).astype(BF16)
        before = jnp.where((row < spot) & (row >= me * block_rows), 1.0, 0.0).astype(BF16)
        which = lax.rem(iota((slots, block_rows), 0), capacity).astype(F32)
        copies[0].wait()
        taken = chosen_ids[...]
        hit = jnp.where((taken >= owner) & (taken < owner + nearby), 1.0, 0.0).astype(BF16)
        mine = jnp.dot(hit, fold, preferred_element_type=F32)
        place = jnp.dot(hit, before, preferred_element_type=F32)
        chosen = jnp.where((mine > 0.5) & (place == which), 1.0, 0.0)
        copies[1].wait()
        placed = jnp.dot(chosen.astype(BF16), part[...], preferred_element_type=F32)
        for step in range(owners_count):
            mine = placed[step * capacity : (step + 1) * capacity]
            if joined:
                out_refs[step][block_rows:, :] = jnp.concatenate(
                    [mine[:, :half], mine[:, half:]], axis=0
                ).astype(BF16)
            else:
                out_refs[2 * step + 1][...] = mine.astype(BF16)
        for copy in copies[2:]:
            copy.wait()

    if joined:
        shapes = [jax.ShapeDtypeStruct((block_rows + 2 * capacity, half), BF16)] * owners_count
    else:
        shapes = [
            jax.ShapeDtypeStruct((block_rows, half), BF16),
            jax.ShapeDtypeStruct((capacity, lane_width), BF16),
        ] * owners_count
    sent = call(
        prepare, "prepare", shapes, [HBM] * 2, [VMEM] * len(shapes),
        (in_hbm(ids), in_hbm(residual_input)),
        scratch=[
            pltpu.VMEM((1, rows), jnp.int32),
            pltpu.VMEM((block_rows, lane_width), BF16),
            pltpu.SemaphoreType.DMA((owners_count + 2,)),
        ],
        moved=2**19,
    )
    per = len(sent) // owners_count
    first_order = list(reversed(range(1, owners_count)))
    arrived = [
        partner(piece, "adapter", step)
        for step in first_order
        for piece in sent[per * step : per * (step + 1)]
    ] + list(sent[:per])

    def place_of(step):
        return first_order.index(step) if step else owners_count - 1

    held = (query_down, value_down, query_weight, key_weight, value_weight)
    made = [
        pltpu.VMEM((2 * low_cols, lane_width), BF16),
        *(pltpu.VMEM(a.shape, a.dtype) for a in held[2:]),
    ]

    def survey(ids_ref, x_ref, length_ref, *refs):
        count = len(held)
        rms_ref, seen_ref, mask_ref, many_ref, ids_copy, x_copy, length_copy, sems = refs[2 * count - 1 :]
        targets = [
            refs[count].at[:low_cols, :], refs[count].at[low_cols:, :],
            *refs[count + 1 : 2 * count - 1],
        ]
        copies = [
            pltpu.make_async_copy(ids_ref, ids_copy, sems.at[0]),
            pltpu.make_async_copy(x_ref, x_copy, sems.at[1]),
            pltpu.make_async_copy(length_ref, length_copy, sems.at[2]),
        ] + [
            pltpu.make_async_copy(refs[i], targets[i], sems.at[3 + i]) for i in range(count)
        ]
        for copy in copies:
            copy.start()
        copies[0].wait()
        me = lax.axis_index("adapter")
        block = jnp.bitwise_xor(me, iota((slots, 1), 0) // capacity)
        seen = slot_map(
            ids_copy[...], jnp.full((slots, 1), me), block, capacity, block_rows, nearby
        )
        spot = iota((rows, rows), 1)
        mirror = jnp.bitwise_xor(me, spot // block_rows) * block_rows + lax.rem(spot, block_rows)
        mirror = jnp.where(iota((rows, rows), 0) == mirror, 1.0, 0.0).astype(BF16)
        seen_ref[...] = jnp.dot(
            seen.astype(BF16), mirror, preferred_element_type=F32
        ).astype(BF16)
        column = lax.rem(iota((slots, 2 * low_cols), 1) // rank, nearby)
        mask = jnp.zeros((slots, 2 * low_cols), F32)
        for near in range(nearby):
            uses = jnp.where(ids_copy[...] == me * nearby + near, seen, 0.0)
            uses = jnp.sum(uses, axis=1, keepdims=True)
            mask = jnp.where(column == near, uses, mask)
        mask_ref[...] = mask
        copies[2].wait()
        same = iota((block_rows, block_rows), 0) == iota((block_rows, block_rows), 1)
        many = jnp.sum(
            jnp.where(same, length_copy[...].astype(F32), 0.0), axis=1, keepdims=True
        )
        many_ref[...] = jnp.broadcast_to(many, many_ref.shape)
        copies[1].wait()
        x = x_copy[...].astype(F32)
        mean = jnp.sum(x * x, axis=1, keepdims=True) * (1.0 / width)
        rms_ref[...] = jnp.broadcast_to(lax.rsqrt(mean + EPS), rms_ref.shape)
        for copy in copies[3:]:
            copy.wait()

    (w_down, w_query, w_key, w_value, row_scale, seen, mask,
     row_length) = call(
        survey, "survey",
        made
        + [
            jax.ShapeDtypeStruct((block_rows, 128), F32),
            jax.ShapeDtypeStruct((slots, rows), BF16),
            jax.ShapeDtypeStruct((slots, 2 * low_cols), F32),
            jax.ShapeDtypeStruct((block_rows, context), F32),
        ],
        [HBM] * (3 + len(held)), [VMEM] * (4 + len(made)),
        (in_hbm(ids), in_hbm(residual_input), in_hbm(cached_length.reshape(1, block_rows)),
         *(in_hbm(a) for a in held)),
        scratch=[
            pltpu.VMEM((1, rows), jnp.int32),
            pltpu.VMEM((block_rows, width), BF16),
            pltpu.VMEM((1, block_rows), jnp.int32),
            pltpu.SemaphoreType.DMA((3 + len(held),)),
        ],
        moved=12 * MIB,
    )

    def base_of(refs, step):
        at = place_of(step)
        return refs[at][:block_rows, :] if joined else refs[2 * at][...]

    def slots_of(refs, step):
        at = place_of(step)
        if not joined:
            return refs[2 * at + 1][...].astype(F32)
        both = refs[at][block_rows:, :].astype(F32)
        return jnp.concatenate([both[:capacity], both[capacity:]], axis=1)

    def lower(gain_ref, mask_ref, down_ref, *refs):
        part_refs, out_ref, half_ref = refs[:-2], refs[-2], refs[-1]
        lane = lax.axis_index("lane")
        scaled = gain_ref[:, pl.ds(pl.multiple_of(lane * lane_width, lane_width), lane_width)]
        taken = jnp.concatenate(
            [slots_of(part_refs, step) for step in range(owners_count)], axis=0
        )
        taken = (taken * scaled).astype(BF16)
        contract = (((1,), (1,)), ((), ()))
        every = mask_ref[...] * lax.dot_general(
            taken, down_ref[...], contract, preferred_element_type=F32
        )
        for at in range(2):
            first = at * low_cols
            picked = every[:, first : first + rank]
            for near in range(1, nearby):
                picked = picked + every[:, first + near * rank : first + (near + 1) * rank]
            out_ref[:, at * rank : (at + 1) * rank] = picked.astype(BF16)
        me = lax.axis_index("adapter")
        first = me * base_width + lax.rem(lane, 2) * half
        scaled = gain_ref[:, pl.ds(pl.multiple_of(first, half), half)]
        for step in range(owners_count):
            half_ref[step * block_rows : (step + 1) * block_rows, :] = (
                base_of(part_refs, step).astype(F32) * scaled
            ).astype(BF16)

    low, near_half = call(
        lower, "lower",
        [
            jax.ShapeDtypeStruct((slots, 2 * rank), BF16),
            jax.ShapeDtypeStruct((rows, half), BF16),
        ],
        [VMEM] * (3 + len(arrived)), [VMEM] * 2,
        (gain, mask, w_down, *arrived),
        moved=MIB,
    )
    far_half = partner(near_half, "lane", 1)
    lows = [low] + [partner(low, "lane", step) for step in range(1, lane_count)]

    def project(near_ref, far_ref, wq_ref, wk_ref, wv_ref, out_ref, x_ref):
        side = lax.rem(lax.axis_index("lane"), 2)
        x_ref[:, pl.ds(pl.multiple_of(side * half, half), half)] = near_ref[...]
        x_ref[:, pl.ds(pl.multiple_of((1 - side) * half, half), half)] = far_ref[...]
        tile = min(1024, query_cols)
        for at in range(0, query_cols, tile):
            out_ref[:, at : at + tile] = jnp.dot(
                x_ref[...], wq_ref[:, at : at + tile], preferred_element_type=F32
            )
        out_ref[:, query_cols : query_cols + kv_cols] = jnp.dot(
            x_ref[...], wk_ref[...], preferred_element_type=F32
        )
        out_ref[:, query_cols + kv_cols :] = jnp.dot(
            x_ref[...], wv_ref[...], preferred_element_type=F32
        )

    based = call(
        project, "project", jax.ShapeDtypeStruct((rows, all_cols), F32),
        [VMEM] * 5, VMEM, (near_half, far_half, w_query, w_key, w_value),
        scratch=[pltpu.VMEM((rows, base_width), BF16)],
        flops=2 * rows * base_width * all_cols, moved=10 * MIB,
    )

    def raise_up(seen_ref, mask_ref, based_ref, uq_ref, uv_ref, *refs):
        low_refs, out_refs = refs[:lane_count], refs[lane_count:]
        total = low_refs[0][...].astype(F32)
        for ref in low_refs[1:]:
            total = total + ref[...].astype(F32)
        spread = [total[:, :rank]] * nearby + [total[:, rank:]] * nearby
        spread = jnp.concatenate(spread, axis=1) * mask_ref[...]
        lowered = lax.dot_general(
            seen_ref[...], spread.astype(BF16), (((0,), (0,)), ((), ())),
            preferred_element_type=F32,
        ).astype(BF16)
        middle = slice(query_cols, query_cols + kv_cols)
        last = slice(query_cols + kv_cols, all_cols)
        tile = min(1024, query_cols)
        pieces = [(slice(at, at + tile), 0, uq_ref, at) for at in range(0, query_cols, tile)]
        pieces.append((last, low_cols, uv_ref, 0))
        for columns, first, weight_ref, at in pieces:
            size = columns.stop - columns.start
            raised = based_ref[:, columns] + ADAPTER_SCALE * jnp.dot(
                lowered[:, first : first + low_cols], weight_ref[:, at : at + size],
                preferred_element_type=F32,
            )
            for step in range(owners_count):
                out_refs[step][:, columns] = raised[
                    step * block_rows : (step + 1) * block_rows
                ].astype(out_refs[step].dtype)
        for step in range(owners_count):
            out_refs[step][:, middle] = based_ref[
                step * block_rows : (step + 1) * block_rows, middle
            ].astype(out_refs[step].dtype)

    parts = call(
        raise_up, "raise_up",
        [
            jax.ShapeDtypeStruct((block_rows, all_cols), BF16 if step else F32)
            for step in range(owners_count)
        ],
        [VMEM] * (5 + lane_count), [VMEM] * owners_count,
        (seen, mask, based, query_up, value_up, *lows),
    )
    parts = [
        partner(parts[step], "adapter", step) for step in [*range(2, owners_count), 1]
    ] + [parts[0]]

    def finish(length_ref, scale_ref, k_ref, v_ref, *refs):
        part_refs = refs[:owners_count]
        out_ref, fresh_ref, sum_ref, q_ref, s_ref, o_ref = refs[owners_count:]
        summed = part_refs[-1][...]
        for ref in part_refs[:-1]:
            summed = summed + ref[...].astype(F32)
        summed = (summed * scale_ref[:, :1]).astype(BF16)
        key_new = summed[:, query_cols : query_cols + kv_cols]
        value_new = summed[:, query_cols + kv_cols :]
        fresh_ref[...] = jnp.stack([key_new, value_new], axis=1)
        sum_ref[...] = summed.astype(F32)
        q_ref[...] = sum_ref[:, :query_cols].reshape(block_rows, heads, head_dim)
        scale = head_dim ** (-0.5)
        twin = 2 * group_size
        spot = iota((twin, context), 1).astype(F32)
        top = iota((twin, 1), 0) < group_size
        keep = jnp.where(top, 1.0, 0.0)

        def pair_of(index):
            return divmod(index, kv_local), divmod(index + 1, kv_local)

        def stacked(index, start):
            (row_a, group_a), (row_b, group_b) = pair_of(index)
            at_a, at_b = start + group_a * head_dim, start + group_b * head_dim
            return jnp.where(
                top,
                sum_ref[row_a : row_a + 1, at_a : at_a + head_dim],
                sum_ref[row_b : row_b + 1, at_b : at_b + head_dim],
            )

        def asked_of(index):
            (row_a, group_a), (row_b, group_b) = pair_of(index)
            return jnp.concatenate(
                [
                    q_ref[row_a, group_a * group_size : (group_a + 1) * group_size, :],
                    q_ref[row_b, group_b * group_size : (group_b + 1) * group_size, :],
                ],
                axis=0,
            )

        def scores_of(index, asked):
            (row_a, group_a), (row_b, group_b) = pair_of(index)
            wide = jnp.concatenate([asked * keep, asked * (1.0 - keep)], axis=1).astype(BF16)
            both = jnp.concatenate([k_ref[row_a, group_a], k_ref[row_b, group_b]], axis=1)
            scores = lax.dot_general(
                wide, both, (((1,), (1,)), ((), ())), preferred_element_type=F32
            )
            length = jnp.where(
                top, length_ref[row_a : row_a + 1, :], length_ref[row_b : row_b + 1, :]
            )
            return jnp.where(spot < length, scores * scale, -jnp.inf)

        def mixed_of(index, weights):
            (row_a, group_a), (row_b, group_b) = pair_of(index)
            both = jnp.concatenate([v_ref[row_a, group_a], v_ref[row_b, group_b]], axis=1)
            mixed = jnp.dot(weights.astype(BF16), both, preferred_element_type=F32)
            return jnp.concatenate(
                [mixed[:group_size, :head_dim], mixed[group_size:, head_dim:]], axis=0
            )

        def put(index, mixed):
            (row_a, group_a), (row_b, group_b) = pair_of(index)
            o_ref[row_a, group_a * group_size : (group_a + 1) * group_size, :] = mixed[:group_size]
            o_ref[row_b, group_b * group_size : (group_b + 1) * group_size, :] = mixed[group_size:]

        pairs = range(0, block_rows * kv_local, 2)
        own = []
        for index in pairs:
            asked = asked_of(index)
            s_ref[index // 2] = scores_of(index, asked)
            own.append(jnp.sum(asked * stacked(index, query_cols), axis=1, keepdims=True))
        own_score = jnp.stack(own) * scale
        scores = s_ref[...]
        peak = jnp.maximum(jnp.max(scores, axis=2, keepdims=True), own_score)
        lifted = jnp.exp(scores - peak)
        own_lift = jnp.exp(own_score - peak)
        inverse = 1.0 / (jnp.sum(lifted, axis=2, keepdims=True) + own_lift)
        s_ref[...] = lifted * inverse
        own_weight = (own_lift * inverse).astype(BF16).astype(F32)
        for index in pairs:
            mixed = mixed_of(index, s_ref[index // 2])
            put(index, mixed + own_weight[index // 2] * stacked(index, query_cols + kv_cols))
        out_ref[...] = o_ref[...].reshape(block_rows, query_cols).astype(BF16)

    attended, fresh = call(
        finish, "finish",
        [
            jax.ShapeDtypeStruct((block_rows, query_cols), BF16),
            jax.ShapeDtypeStruct((block_rows, 2, kv_cols), BF16),
        ],
        [VMEM] * (4 + owners_count), [VMEM] * 2,
        (row_length, row_scale, cached_key_rows, cached_value_rows, *parts),
        scratch=[
            pltpu.VMEM((block_rows, all_cols), F32),
            pltpu.VMEM((block_rows, heads, head_dim), F32),
            pltpu.VMEM((block_rows * kv_local // 2, 2 * group_size, context), F32),
            pltpu.VMEM((block_rows, heads, head_dim), F32),
        ],
    )
    return (attended, fresh)


def solution(mesh):
    in_specs = (
        P(("groups", "adapter"), None),
        P(),
        P("adapter", "lane"),
        P("adapter", "lane"),
        P("adapter", "lane"),
        P("adapter", "lane", None),
        P("adapter", None, "lane"),
        P("adapter", "lane", None),
        P("adapter", None, "lane"),
        P(("groups", "adapter"), "lane", None, None),
        P(("groups", "adapter"), "lane", None, None),
        P("groups"),
        P(("groups", "adapter")),
    )
    out_specs = (P(("groups", "adapter"), "lane"), P(("groups", "adapter"), None, "lane"))
    return jax.shard_map(
        on_device, mesh=mesh, in_specs=in_specs, out_specs=out_specs, check_vma=False
    )
```

```python
import jax
import jax.numpy as jnp
from jax import lax
from jax.experimental import pallas as pl
from jax.experimental.pallas import tpu as pltpu
from jax.sharding import PartitionSpec as P

EPS = 1e-05
ADAPTER_SCALE = 0.5
MIB = 2**20
F32 = jnp.float32
BF16 = jnp.bfloat16
VMEM = pl.BlockSpec(memory_space=pltpu.VMEM)
HBM = pl.BlockSpec(memory_space=pltpu.HBM)


def partner(array, axis, step):
    count = lax.axis_size(axis)
    return lax.ppermute(array, axis, [(i, i ^ step) for i in range(count)])


def call(body, name, outs, in_specs, out_specs, args, scratch=(), limit=16, flops=0, moved=0):
    return pl.pallas_call(
        body,
        name=name,
        out_shape=outs,
        in_specs=in_specs,
        out_specs=out_specs,
        scratch_shapes=scratch,
        compiler_params=pltpu.CompilerParams(vmem_limit_bytes=limit * MIB),
        cost_estimate=pl.CostEstimate(flops=flops, bytes_accessed=moved, transcendentals=0),
    )(*args)


def in_hbm(array):
    return pltpu.with_memory_space_constraint(array, pltpu.HBM)


def iota(shape, axis):
    return lax.broadcasted_iota(jnp.int32, shape, axis)


def slot_map(ids, owner, block, capacity, block_rows, nearby):
    slots, rows = owner.shape[0], ids.shape[1]
    first = owner * nearby
    spot = iota((slots, rows), 1)
    hit = (ids >= first) & (ids < first + nearby)
    hit = hit & (spot >= block * block_rows) & (spot < (block + 1) * block_rows)
    before = (iota((rows, rows), 0) < iota((rows, rows), 1)).astype(BF16)
    place = jnp.dot(
        jnp.where(hit, 1.0, 0.0).astype(BF16), before, preferred_element_type=F32
    )
    which = lax.rem(iota((slots, rows), 0), capacity).astype(F32)
    return jnp.where(hit & (place == which), 1.0, 0.0)


def on_device(
    residual_input,
    attention_norm_gain,
    query_weight,
    key_weight,
    value_weight,
    query_down_weight,
    query_up_weight,
    value_down_weight,
    value_up_weight,
    cached_key_rows,
    cached_value_rows,
    row_adapter_index,
    cached_length,
):
    owners_count = lax.axis_size("adapter")
    lane_count = lax.axis_size("lane")
    block_rows, width = residual_input.shape
    nearby, _, rank = query_down_weight.shape
    capacity = max(2, 2 * block_rows // owners_count)
    lane_width = width // lane_count
    base_width = width // owners_count
    query_cols = query_weight.shape[1]
    kv_cols = key_weight.shape[1]
    all_cols = query_cols + 2 * kv_cols
    slots = owners_count * capacity
    rows = owners_count * block_rows
    low_cols = nearby * rank
    half = base_width // 2
    joined = 2 * half == lane_width
    kv_local, context, head_dim = cached_key_rows.shape[1:]
    group_size = query_cols // head_dim // kv_local
    heads = kv_local * group_size

    ids = row_adapter_index.reshape(1, rows)
    gain = attention_norm_gain.reshape(1, width)
    query_down = jnp.swapaxes(query_down_weight, 1, 2).reshape(low_cols, lane_width)
    value_down = jnp.swapaxes(value_down_weight, 1, 2).reshape(low_cols, lane_width)
    query_up = query_up_weight.reshape(low_cols, query_cols)
    value_up = value_up_weight.reshape(low_cols, kv_cols)

    def prepare(ids_ref, x_ref, *refs):
        out_refs, chosen_ids, part, sems = refs[:-3], refs[-3], refs[-2], refs[-1]
        me = lax.axis_index("adapter")
        lane = lax.axis_index("lane")
        lane_at = pl.ds(pl.multiple_of(lane * lane_width, lane_width), lane_width)
        copies = [
            pltpu.make_async_copy(ids_ref, chosen_ids, sems.at[owners_count]),
            pltpu.make_async_copy(x_ref.at[:, lane_at], part, sems.at[owners_count + 1]),
        ]
        for step in range(owners_count):
            other = jnp.bitwise_xor(me, step)
            at = pl.ds(pl.multiple_of(other * base_width + lax.rem(lane, 2) * half, half), half)
            target = out_refs[step].at[:block_rows, :] if joined else out_refs[2 * step]
            copies.append(pltpu.make_async_copy(x_ref.at[:, at], target, sems.at[step]))
        for copy in copies:
            copy.start()
        owner = jnp.bitwise_xor(me, iota((slots, rows), 0) // capacity) * nearby
        row, spot = iota((rows, block_rows), 0), iota((rows, block_rows), 1) + me * block_rows
        fold = jnp.where(row == spot, 1.0, 0.0).astype(BF16)
        before = jnp.where((row < spot) & (row >= me * block_rows), 1.0, 0.0).astype(BF16)
        which = lax.rem(iota((slots, block_rows), 0), capacity).astype(F32)
        copies[0].wait()
        taken = chosen_ids[...]
        hit = jnp.where((taken >= owner) & (taken < owner + nearby), 1.0, 0.0).astype(BF16)
        mine = jnp.dot(hit, fold, preferred_element_type=F32)
        place = jnp.dot(hit, before, preferred_element_type=F32)
        chosen = jnp.where((mine > 0.5) & (place == which), 1.0, 0.0)
        copies[1].wait()
        placed = jnp.dot(chosen.astype(BF16), part[...], preferred_element_type=F32)
        for step in range(owners_count):
            mine = placed[step * capacity : (step + 1) * capacity]
            if joined:
                out_refs[step][block_rows:, :] = jnp.concatenate(
                    [mine[:, :half], mine[:, half:]], axis=0
                ).astype(BF16)
            else:
                out_refs[2 * step + 1][...] = mine.astype(BF16)
        for copy in copies[2:]:
            copy.wait()

    if joined:
        shapes = [jax.ShapeDtypeStruct((block_rows + 2 * capacity, half), BF16)] * owners_count
    else:
        shapes = [
            jax.ShapeDtypeStruct((block_rows, half), BF16),
            jax.ShapeDtypeStruct((capacity, lane_width), BF16),
        ] * owners_count
    sent = call(
        prepare, "prepare", shapes, [HBM] * 2, [VMEM] * len(shapes),
        (in_hbm(ids), in_hbm(residual_input)),
        scratch=[
            pltpu.VMEM((1, rows), jnp.int32),
            pltpu.VMEM((block_rows, lane_width), BF16),
            pltpu.SemaphoreType.DMA((owners_count + 2,)),
        ],
        moved=2**19,
    )
    per = len(sent) // owners_count
    first_order = list(reversed(range(1, owners_count)))
    arrived = [
        partner(piece, "adapter", step)
        for step in first_order
        for piece in sent[per * step : per * (step + 1)]
    ] + list(sent[:per])

    def place_of(step):
        return first_order.index(step) if step else owners_count - 1

    held = (query_down, value_down, query_weight, key_weight, value_weight)
    made = [
        pltpu.VMEM((2 * low_cols, lane_width), BF16),
        *(pltpu.VMEM(a.shape, a.dtype) for a in held[2:]),
    ]

    def survey(ids_ref, x_ref, length_ref, *refs):
        count = len(held)
        rms_ref, seen_ref, mask_ref, many_ref, ids_copy, x_copy, length_copy, sems = refs[2 * count - 1 :]
        targets = [
            refs[count].at[:low_cols, :], refs[count].at[low_cols:, :],
            *refs[count + 1 : 2 * count - 1],
        ]
        copies = [
            pltpu.make_async_copy(ids_ref, ids_copy, sems.at[0]),
            pltpu.make_async_copy(x_ref, x_copy, sems.at[1]),
            pltpu.make_async_copy(length_ref, length_copy, sems.at[2]),
        ] + [
            pltpu.make_async_copy(refs[i], targets[i], sems.at[3 + i]) for i in range(count)
        ]
        for copy in copies:
            copy.start()
        copies[0].wait()
        me = lax.axis_index("adapter")
        block = jnp.bitwise_xor(me, iota((slots, 1), 0) // capacity)
        seen = slot_map(
            ids_copy[...], jnp.full((slots, 1), me), block, capacity, block_rows, nearby
        )
        spot = iota((rows, rows), 1)
        mirror = jnp.bitwise_xor(me, spot // block_rows) * block_rows + lax.rem(spot, block_rows)
        mirror = jnp.where(iota((rows, rows), 0) == mirror, 1.0, 0.0).astype(BF16)
        seen_ref[...] = jnp.dot(
            seen.astype(BF16), mirror, preferred_element_type=F32
        ).astype(BF16)
        column = lax.rem(iota((slots, 2 * low_cols), 1) // rank, nearby)
        mask = jnp.zeros((slots, 2 * low_cols), F32)
        for near in range(nearby):
            uses = jnp.where(ids_copy[...] == me * nearby + near, seen, 0.0)
            uses = jnp.sum(uses, axis=1, keepdims=True)
            mask = jnp.where(column == near, uses, mask)
        mask_ref[...] = mask
        copies[2].wait()
        same = iota((block_rows, block_rows), 0) == iota((block_rows, block_rows), 1)
        many = jnp.sum(
            jnp.where(same, length_copy[...].astype(F32), 0.0), axis=1, keepdims=True
        )
        many_ref[...] = jnp.broadcast_to(many, many_ref.shape)
        copies[1].wait()
        x = x_copy[...].astype(F32)
        mean = jnp.sum(x * x, axis=1, keepdims=True) * (1.0 / width)
        rms_ref[...] = jnp.broadcast_to(lax.rsqrt(mean + EPS), rms_ref.shape)
        for copy in copies[3:]:
            copy.wait()

    (w_down, w_query, w_key, w_value, row_scale, seen, mask,
     row_length) = call(
        survey, "survey",
        made
        + [
            jax.ShapeDtypeStruct((block_rows, 128), F32),
            jax.ShapeDtypeStruct((slots, rows), BF16),
            jax.ShapeDtypeStruct((slots, 2 * low_cols), F32),
            jax.ShapeDtypeStruct((block_rows, context), F32),
        ],
        [HBM] * (3 + len(held)), [VMEM] * (4 + len(made)),
        (in_hbm(ids), in_hbm(residual_input), in_hbm(cached_length.reshape(1, block_rows)),
         *(in_hbm(a) for a in held)),
        scratch=[
            pltpu.VMEM((1, rows), jnp.int32),
            pltpu.VMEM((block_rows, width), BF16),
            pltpu.VMEM((1, block_rows), jnp.int32),
            pltpu.SemaphoreType.DMA((3 + len(held),)),
        ],
        moved=12 * MIB,
    )

    def base_of(refs, step):
        at = place_of(step)
        return refs[at][:block_rows, :] if joined else refs[2 * at][...]

    def slots_of(refs, step):
        at = place_of(step)
        if not joined:
            return refs[2 * at + 1][...].astype(F32)
        both = refs[at][block_rows:, :].astype(F32)
        return jnp.concatenate([both[:capacity], both[capacity:]], axis=1)

    def lower(gain_ref, mask_ref, down_ref, *refs):
        part_refs, out_ref, half_ref = refs[:-2], refs[-2], refs[-1]
        lane = lax.axis_index("lane")
        scaled = gain_ref[:, pl.ds(pl.multiple_of(lane * lane_width, lane_width), lane_width)]
        taken = jnp.concatenate(
            [slots_of(part_refs, step) for step in range(owners_count)], axis=0
        )
        taken = (taken * scaled).astype(BF16)
        contract = (((1,), (1,)), ((), ()))
        every = mask_ref[...] * lax.dot_general(
            taken, down_ref[...], contract, preferred_element_type=F32
        )
        for at in range(2):
            first = at * low_cols
            picked = every[:, first : first + rank]
            for near in range(1, nearby):
                picked = picked + every[:, first + near * rank : first + (near + 1) * rank]
            out_ref[:, at * rank : (at + 1) * rank] = picked.astype(BF16)
        me = lax.axis_index("adapter")
        first = me * base_width + lax.rem(lane, 2) * half
        scaled = gain_ref[:, pl.ds(pl.multiple_of(first, half), half)]
        for step in range(owners_count):
            half_ref[step * block_rows : (step + 1) * block_rows, :] = (
                base_of(part_refs, step).astype(F32) * scaled
            ).astype(BF16)

    low, near_half = call(
        lower, "lower",
        [
            jax.ShapeDtypeStruct((slots, 2 * rank), BF16),
            jax.ShapeDtypeStruct((rows, half), BF16),
        ],
        [VMEM] * (3 + len(arrived)), [VMEM] * 2,
        (gain, mask, w_down, *arrived),
        moved=MIB,
    )
    far_half = partner(near_half, "lane", 1)
    lows = [low] + [partner(low, "lane", step) for step in range(1, lane_count)]

    def project(near_ref, far_ref, wq_ref, wk_ref, wv_ref, out_ref, x_ref):
        side = lax.rem(lax.axis_index("lane"), 2)
        x_ref[:, pl.ds(pl.multiple_of(side * half, half), half)] = near_ref[...]
        x_ref[:, pl.ds(pl.multiple_of((1 - side) * half, half), half)] = far_ref[...]
        tile = min(1024, query_cols)
        for at in range(0, query_cols, tile):
            out_ref[:, at : at + tile] = jnp.dot(
                x_ref[...], wq_ref[:, at : at + tile], preferred_element_type=F32
            )
        out_ref[:, query_cols : query_cols + kv_cols] = jnp.dot(
            x_ref[...], wk_ref[...], preferred_element_type=F32
        )
        out_ref[:, query_cols + kv_cols :] = jnp.dot(
            x_ref[...], wv_ref[...], preferred_element_type=F32
        )

    based = call(
        project, "project", jax.ShapeDtypeStruct((rows, all_cols), F32),
        [VMEM] * 5, VMEM, (near_half, far_half, w_query, w_key, w_value),
        scratch=[pltpu.VMEM((rows, base_width), BF16)],
        flops=2 * rows * base_width * all_cols, moved=10 * MIB,
    )

    def raise_up(seen_ref, mask_ref, based_ref, uq_ref, uv_ref, *refs):
        low_refs, out_refs = refs[:lane_count], refs[lane_count:]
        total = low_refs[0][...].astype(F32)
        for ref in low_refs[1:]:
            total = total + ref[...].astype(F32)
        spread = [total[:, :rank]] * nearby + [total[:, rank:]] * nearby
        spread = jnp.concatenate(spread, axis=1) * mask_ref[...]
        lowered = lax.dot_general(
            seen_ref[...], spread.astype(BF16), (((0,), (0,)), ((), ())),
            preferred_element_type=F32,
        ).astype(BF16)
        middle = slice(query_cols, query_cols + kv_cols)
        last = slice(query_cols + kv_cols, all_cols)
        tile = min(1024, query_cols)
        pieces = [(slice(at, at + tile), 0, uq_ref, at) for at in range(0, query_cols, tile)]
        pieces.append((last, low_cols, uv_ref, 0))
        for columns, first, weight_ref, at in pieces:
            size = columns.stop - columns.start
            raised = based_ref[:, columns] + ADAPTER_SCALE * jnp.dot(
                lowered[:, first : first + low_cols], weight_ref[:, at : at + size],
                preferred_element_type=F32,
            )
            for step in range(owners_count):
                out_refs[step][:, columns] = raised[
                    step * block_rows : (step + 1) * block_rows
                ].astype(out_refs[step].dtype)
        for step in range(owners_count):
            out_refs[step][:, middle] = based_ref[
                step * block_rows : (step + 1) * block_rows, middle
            ].astype(out_refs[step].dtype)

    parts = call(
        raise_up, "raise_up",
        [
            jax.ShapeDtypeStruct((block_rows, all_cols), BF16 if step else F32)
            for step in range(owners_count)
        ],
        [VMEM] * (5 + lane_count), [VMEM] * owners_count,
        (seen, mask, based, query_up, value_up, *lows),
    )
    parts = [
        partner(parts[step], "adapter", step) for step in [*range(2, owners_count), 1]
    ] + [parts[0]]

    def finish(length_ref, scale_ref, k_ref, v_ref, *refs):
        part_refs = refs[:owners_count]
        out_ref, fresh_ref, sum_ref, q_ref, s_ref, o_ref = refs[owners_count:]
        summed = part_refs[-1][...]
        for ref in part_refs[:-1]:
            summed = summed + ref[...].astype(F32)
        summed = (summed * scale_ref[:, :1]).astype(BF16)
        key_new = summed[:, query_cols : query_cols + kv_cols]
        value_new = summed[:, query_cols + kv_cols :]
        fresh_ref[...] = jnp.stack([key_new, value_new], axis=1)
        sum_ref[...] = summed.astype(F32)
        q_ref[...] = sum_ref[:, :query_cols].reshape(block_rows, heads, head_dim)
        scale = head_dim ** (-0.5)
        twin = 2 * group_size
        spot = iota((twin, context), 1).astype(F32)
        top = iota((twin, 1), 0) < group_size
        keep = jnp.where(top, 1.0, 0.0)

        def pair_of(index):
            return divmod(index, kv_local), divmod(index + 1, kv_local)

        def stacked(index, start):
            (row_a, group_a), (row_b, group_b) = pair_of(index)
            at_a, at_b = start + group_a * head_dim, start + group_b * head_dim
            return jnp.where(
                top,
                sum_ref[row_a : row_a + 1, at_a : at_a + head_dim],
                sum_ref[row_b : row_b + 1, at_b : at_b + head_dim],
            )

        def asked_of(index):
            (row_a, group_a), (row_b, group_b) = pair_of(index)
            return jnp.concatenate(
                [
                    q_ref[row_a, group_a * group_size : (group_a + 1) * group_size, :],
                    q_ref[row_b, group_b * group_size : (group_b + 1) * group_size, :],
                ],
                axis=0,
            )

        def scores_of(index, asked):
            (row_a, group_a), (row_b, group_b) = pair_of(index)
            wide = jnp.concatenate([asked * keep, asked * (1.0 - keep)], axis=1).astype(BF16)
            both = jnp.concatenate([k_ref[row_a, group_a], k_ref[row_b, group_b]], axis=1)
            scores = lax.dot_general(
                wide, both, (((1,), (1,)), ((), ())), preferred_element_type=F32
            )
            length = jnp.where(
                top, length_ref[row_a : row_a + 1, :], length_ref[row_b : row_b + 1, :]
            )
            return jnp.where(spot < length, scores * scale, -jnp.inf)

        def mixed_of(index, weights):
            (row_a, group_a), (row_b, group_b) = pair_of(index)
            both = jnp.concatenate([v_ref[row_a, group_a], v_ref[row_b, group_b]], axis=1)
            mixed = jnp.dot(weights.astype(BF16), both, preferred_element_type=F32)
            return jnp.concatenate(
                [mixed[:group_size, :head_dim], mixed[group_size:, head_dim:]], axis=0
            )

        def put(index, mixed):
            (row_a, group_a), (row_b, group_b) = pair_of(index)
            o_ref[row_a, group_a * group_size : (group_a + 1) * group_size, :] = mixed[:group_size]
            o_ref[row_b, group_b * group_size : (group_b + 1) * group_size, :] = mixed[group_size:]

        pairs = range(0, block_rows * kv_local, 2)
        own = []
        for index in pairs:
            asked = asked_of(index)
            s_ref[index // 2] = scores_of(index, asked)
            own.append(jnp.sum(asked * stacked(index, query_cols), axis=1, keepdims=True))
        own_score = jnp.stack(own) * scale
        scores = s_ref[...]
        peak = jnp.maximum(jnp.max(scores, axis=2, keepdims=True), own_score)
        lifted = jnp.exp(scores - peak)
        own_lift = jnp.exp(own_score - peak)
        inverse = 1.0 / (jnp.sum(lifted, axis=2, keepdims=True) + own_lift)
        s_ref[...] = lifted
        own_weight = own_lift.astype(BF16).astype(F32)
        for index in pairs:
            mixed = mixed_of(index, s_ref[index // 2])
            mixed = mixed + own_weight[index // 2] * stacked(index, query_cols + kv_cols)
            put(index, mixed * inverse[index // 2])
        out_ref[...] = o_ref[...].reshape(block_rows, query_cols).astype(BF16)

    attended, fresh = call(
        finish, "finish",
        [
            jax.ShapeDtypeStruct((block_rows, query_cols), BF16),
            jax.ShapeDtypeStruct((block_rows, 2, kv_cols), BF16),
        ],
        [VMEM] * (4 + owners_count), [VMEM] * 2,
        (row_length, row_scale, cached_key_rows, cached_value_rows, *parts),
        scratch=[
            pltpu.VMEM((block_rows, all_cols), F32),
            pltpu.VMEM((block_rows, heads, head_dim), F32),
            pltpu.VMEM((block_rows * kv_local // 2, 2 * group_size, context), F32),
            pltpu.VMEM((block_rows, heads, head_dim), F32),
        ],
    )
    return (attended, fresh)


def solution(mesh):
    in_specs = (
        P(("groups", "adapter"), None),
        P(),
        P("adapter", "lane"),
        P("adapter", "lane"),
        P("adapter", "lane"),
        P("adapter", "lane", None),
        P("adapter", None, "lane"),
        P("adapter", "lane", None),
        P("adapter", None, "lane"),
        P(("groups", "adapter"), "lane", None, None),
        P(("groups", "adapter"), "lane", None, None),
        P("groups"),
        P(("groups", "adapter")),
    )
    out_specs = (P(("groups", "adapter"), "lane"), P(("groups", "adapter"), None, "lane"))
    return jax.shard_map(
        on_device, mesh=mesh, in_specs=in_specs, out_specs=out_specs, check_vma=False
    )
```
